256 devices in a mesh: ctx: 16 (over x, y), exp: 16 (over z, core).
Axes of the slice: x: 4, y: 4, z: 8, core: 2. Of those that a mesh axis runs over, the one named last changes fastest.
Arguments:
- inner_input: bfloat16 [2048, 8192], P('ctx', 'exp'), may hold values from -6 to 6
- gate_input: bfloat16 [2048, 8192], P('ctx', 'exp'), may hold values from -6 to 6
- step_codes: int32 [2048, 8192], P('ctx', 'exp'), may hold values from 4 to 16384
- conv_weight: float32 [4, 8192], P(None, 'exp'), may hold values from -3 to 3
- conv_bias: float32 [8192], P('exp'), may hold values from -3 to 3
- decay_rates: float32 [16, 8192], P(None, 'exp')
- skip_gain: float32 [8192], P('exp'), may hold values from 0.5 to 1.5
- state_proj: bfloat16 [8192, 32], P('exp'), may hold values from -0.0625 to 0.0625
- out_proj: bfloat16 [8192, 4096], P('exp'), may hold values from -0.0625 to 0.0625
- residual: bfloat16 [2048, 4096], P(('ctx', 'exp')), may hold values from -6 to 6
- norm_gain: float32 [4096], replicated, may hold values from 0.25 to 1.75
- expert_ids: int32 [2048, 2], P(('ctx', 'exp')), may hold values from 0 to 15, all different within a row; in each aligned block of 8 rows (0 to 7, 8 to 15, ...) at most 2 rows name the same one
- gate_codes: int32 [2048, 2], P(('ctx', 'exp')), may hold values from 1 to 255
- up_weight: bfloat16 [16, 4096, 8192], P('exp', None, 'ctx'), may hold values from -0.09375 to 0.09375
- down_weight: bfloat16 [16, 8192, 4096], P('exp', 'ctx'), may hold values from -0.0625 to 0.0625
Outputs:
- layer_out: bfloat16 [2048, 4096], P(('ctx', 'exp'))
The draws below stay inside these ranges and needn't reach their ends.
Inputs may be any that keep to these rules, and one draw needn't show every extreme that they name: `expert_ids`: each row names 2 different experts. In each aligned block of 8 rows (the tokens of one device) no expert is named by more than 2 rows.
All inputs are finite; a program needn't handle non-finite values.
Results may differ from the reference program's by a relative error of at most 0.028.
Values may be sent and summed in bfloat16 or wider, within the bound.
No kernel may reach another device: no remote copies, remote signals or barrier semaphores. Data moves between devices by JAX's collectives and lax.ppermute only.
A program may use at most 128 MiB of HBM per device.

```python
import math
import jax
import jax.numpy as jnp
import numpy as np
from jax import lax

D = 4096
INNER = 8192
NSTATE = 16
KCONV = 4
TOPK = 2
FF = 8192
EXPERTS = 16
TOKEN_COUNT = 2048
ROWS = 8
CAP = 2
FFL = 512
ICH = 512
N_CTX = 16
N_EXP = 16


def draw_step_codes(key, part):
    key = jax.random.fold_in(key, 11)
    symbol_key, spike_key = jax.random.split(key)
    symbol_values = jax.random.randint(symbol_key, (TOKEN_COUNT, INNER), 4, 14)
    spike_rows = jax.random.randint(spike_key, (2,), 0, TOKEN_COUNT)
    token_places = jnp.arange(TOKEN_COUNT)
    spike_flag = jnp.any(token_places[:, None] == spike_rows[None, :], axis=1)
    return jnp.where(spike_flag[:, None], 8 * TOKEN_COUNT, symbol_values).astype(jnp.int32)


def draw_decay_rates(key, part):
    key = jax.random.fold_in(key, 23)
    pick_key, slow_key, fast_key = jax.random.split(key, 3)
    keep_share = 0.5
    chosen = jax.random.uniform(pick_key, (NSTATE, INNER), jnp.float32) < keep_share
    slow_rates = jnp.exp(jax.random.uniform(slow_key, (NSTATE, INNER), jnp.float32, math.log(6.0), math.log(18.0))) / TOKEN_COUNT
    fast_rates = jnp.exp(jax.random.uniform(fast_key, (NSTATE, INNER), jnp.float32, math.log(0.6), 0.0))
    return jnp.where(chosen, slow_rates, fast_rates).astype(jnp.float32)


def place_ends(entries, stream_key, low, top_value):
    longest = entries.shape.index(max(entries.shape))
    spots = []
    for shift in (0, 1):
        where = [jax.random.randint(jax.random.fold_in(stream_key, axis), (), 0, length) for axis, length in enumerate(entries.shape)]
        where[longest] = (where[longest] + shift) % entries.shape[longest]
        spots.append(tuple(where))
    return entries.at[spots[0]].set(low).at[spots[1]].set(top_value)


def block_levels(rng, shape, cuts, least, high):
    def one(dim, shards_of):
        steps = jax.random.uniform(jax.random.fold_in(jax.random.fold_in(rng, 6), dim), (shards_of,), jnp.float32, least / len(cuts), high / len(cuts))
        return jnp.repeat(jnp.exp(steps), shape[dim] // shards_of).reshape((-1,) + (1,) * (len(shape) - dim - 1))

    loudness = one(*cuts[0])
    for cut in cuts[1:]:
        loudness = loudness * one(*cut)
    return loudness


def deal_out(stream_key, own, number, rows, amount, top, limit, skew):
    sequence = jax.random.permutation(stream_key, amount)
    crowded, common = shares(amount, rows * top, limit, skew, True), shares(amount, rows * top, limit, skew, False)
    places = jnp.arange(amount)

    def named(lengths, offset_by):
        used = int((lengths > 0).sum())
        fixed = max(1, used // 4)
        shifted = fixed + (places - fixed + offset_by * (used - fixed)) % max(1, amount - fixed)
        return jnp.zeros((amount,), jnp.int32).at[sequence[jnp.where(places < fixed, places, shifted)]].set(jnp.asarray(lengths, jnp.int32))

    lengths = jnp.where(number % 4 == 0, named(crowded, number // 4), named(common, number - number // 4 - 1))
    mixed = jax.random.permutation(jax.random.fold_in(own, 3), amount)
    giver, taker = mixed[0:amount // 2 * 2:2], mixed[1:amount // 2 * 2:2]
    room = jnp.minimum(lengths[giver] - 1, limit - lengths[taker]) // 2
    room = jnp.where((giver == sequence[0]) | (taker == sequence[0]) | (lengths[taker] == 0), 0, jnp.maximum(room, 0))
    shifted = jax.random.randint(jax.random.fold_in(own, 4), (amount // 2,), 0, 1 << 20) % (room + 1)
    lengths = lengths.at[giver].add(-shifted).at[taker].add(shifted)
    members = jnp.searchsorted(jnp.cumsum(lengths), jnp.arange(rows * top), side="right").astype(jnp.int32)
    grid = members.reshape(top, rows).T
    grid = grid[jax.random.permutation(jax.random.fold_in(own, 1), rows)]
    offset_by = jax.random.randint(jax.random.fold_in(own, 2), (rows, 1), 0, top)
    return jnp.take_along_axis(grid, (jnp.arange(top)[None, :] + offset_by) % top, axis=1)


def shares(amount, total, most, slope, full):
    portions = [(1 << 20) // math.isqrt(grade ** slope) + 1 for grade in range(1, amount + 1)]
    largest = most if full else min(most, max(-(-total // amount), total * portions[0] // sum(portions)))
    least = 1 if total - largest >= amount - 1 else 0
    holding, spare = [largest] + [least] * (amount - 1), total - largest - least * (amount - 1)
    while spare > 0:
        movable = [i for i in range(1, amount) if holding[i] < largest] or [i for i in range(1, amount) if holding[i] < most]
        mass, budget = sum([portions[i] for i in movable]), spare
        for i in movable:
            more = min(most - holding[i], max(1, budget * portions[i] // mass), spare)
            holding[i] = holding[i] + more
            spare = spare - more
    return np.array(holding)


def centred(rng, dims, spread, limit, cuts=(), held_as=jnp.bfloat16):
    gain = block_levels(rng, dims, cuts, -0.22, 0.18) if cuts else 1.0
    result = jax.random.normal(rng, dims, jnp.float32) * spread * gain
    return jnp.minimum(jnp.maximum(result, -limit), limit).astype(held_as)


def setup_inputs(seed: int = 0) -> dict:
    key_of = jax.random.split(jax.random.key(seed), 16)
    inner_input = centred(key_of[0], (TOKEN_COUNT, INNER), 1.0, 6.0, ((0, 16), (1, 16)))
    gate_input = centred(key_of[1], (TOKEN_COUNT, INNER), 1.0, 6.0, ((0, 16), (1, 16)))
    step_codes = draw_step_codes(jax.random.fold_in(key_of[15], 71), 0)
    conv_weight = centred(key_of[3], (KCONV, INNER), 0.5, 3.0, ((1, 16),), jnp.float32)
    conv_bias = centred(key_of[4], (INNER,), 0.5, 3.0, ((0, 16),), jnp.float32)
    decay_rates = draw_decay_rates(jax.random.fold_in(key_of[15], 71), 0)
    skip_gain = jnp.clip(0.5 + 1.0 * jax.random.uniform(key_of[6], (INNER,), jnp.float32) ** block_levels(key_of[6], (INNER,), ((0, 16),), -0.2, 0.2), 0.5, 1.5)
    state_proj = centred(key_of[7], (INNER, 2 * NSTATE), INNER ** -0.5, 0.0625, ((0, 16),))
    out_proj = centred(key_of[8], (INNER, D), INNER ** -0.5, 0.0625, ((0, 16),))
    residual = centred(key_of[9], (TOKEN_COUNT, D), 1.0, 6.0, ((0, 256),))
    norm_gain = jnp.clip(jax.random.uniform(key_of[10], (D,), jnp.float32, 0.25, 1.75), 0.25, 1.75)
    expert_ids_keys = jax.random.split(jax.random.fold_in(key_of[11], 1), TOKEN_COUNT // ROWS)
    expert_ids_turns = jax.random.permutation(jax.random.fold_in(key_of[11], 3), TOKEN_COUNT // ROWS)
    expert_ids = jax.vmap(lambda own, number: deal_out(jax.random.fold_in(key_of[11], 2), own, number, ROWS, EXPERTS, TOPK, CAP, 2))(expert_ids_keys, expert_ids_turns).reshape((TOKEN_COUNT, TOPK))
    gate_codes = place_ends(jax.random.randint(key_of[12], (TOKEN_COUNT, TOPK), 1, 256), jax.random.fold_in(key_of[12], 1), 1, 255).astype(jnp.int32)
    up_weight = centred(key_of[13], (EXPERTS, D, FF), D ** -0.5, 0.09375, ((0, 16), (2, 16)))
    down_weight = centred(key_of[14], (EXPERTS, FF, D), FF ** -0.5, 0.0625, ((0, 16), (1, 16)))
    return {"inner_input": inner_input, "gate_input": gate_input, "step_codes": step_codes, "conv_weight": conv_weight, "conv_bias": conv_bias, "decay_rates": decay_rates, "skip_gain": skip_gain, "state_proj": state_proj, "out_proj": out_proj, "residual": residual, "norm_gain": norm_gain, "expert_ids": expert_ids, "gate_codes": gate_codes, "up_weight": up_weight, "down_weight": down_weight}


def reference(inner_input, gate_input, step_codes, conv_weight, conv_bias, decay_rates, skip_gain, state_proj, out_proj, residual, norm_gain, expert_ids, gate_codes, up_weight, down_weight):
    padded = jnp.concatenate([jnp.zeros((KCONV - 1, INNER), jnp.float32), inner_input.astype(jnp.float32)], axis=0)
    convolved = conv_weight[0] * padded[0:TOKEN_COUNT]
    for offset in range(1, KCONV):
        convolved = convolved + conv_weight[offset] * padded[offset:offset + TOKEN_COUNT]
    convolved = convolved + conv_bias
    signal = jax.nn.silu(convolved)
    maps = jnp.dot(signal.astype(jnp.bfloat16), state_proj, preferred_element_type=jnp.float32)
    input_map = maps[:, :NSTATE]
    output_map = maps[:, NSTATE:]
    step_sizes = step_codes.astype(jnp.float32) * (1.0 / 256.0)
    drive_term = jnp.minimum(step_sizes, 1.0) * signal

    def advance(state, pieces):
        step_row, drive_row, input_row, output_row = pieces
        state = jnp.exp(-step_row[None, :] * decay_rates) * state + input_row[:, None] * drive_row[None, :]
        return (state, lax.optimization_barrier(jnp.sum(output_row[:, None] * state, axis=0)))
    ignored, state_out = lax.scan(advance, jnp.zeros((NSTATE, INNER), jnp.float32), (step_sizes, drive_term, input_map, output_map))
    gated_out = ((state_out + skip_gain * signal) * jax.nn.silu(gate_input.astype(jnp.float32))).astype(jnp.bfloat16)

    def add_channels(running, block_number):
        gated_part = lax.dynamic_slice_in_dim(gated_out, block_number * ICH, ICH, 1)
        proj_part = lax.dynamic_slice_in_dim(out_proj, block_number * ICH, ICH, 0)
        block_sum = lax.optimization_barrier(jnp.dot(gated_part, proj_part, preferred_element_type=jnp.float32).astype(jnp.bfloat16))
        return (running + block_sum.astype(jnp.float32), None)
    mamba_out, unused_blocks = lax.scan(add_channels, jnp.zeros((TOKEN_COUNT, D), jnp.float32), jnp.arange(N_EXP, dtype=jnp.int32))
    stream = (residual.astype(jnp.float32) + mamba_out).astype(jnp.bfloat16)
    stream_wide = stream.astype(jnp.float32)
    normed = (stream_wide * lax.rsqrt(lax.optimization_barrier(jnp.mean(stream_wide * stream_wide, axis=-1, keepdims=True)) + 1e-05) * norm_gain).astype(jnp.bfloat16)
    blocks = TOKEN_COUNT // ROWS
    onehot = (expert_ids[:, :, None] == jnp.arange(EXPERTS, dtype=jnp.int32)[None, None, :]).astype(jnp.int32)
    onehot = onehot.reshape(blocks, ROWS * TOPK, EXPERTS)
    before = jnp.cumsum(onehot, axis=1) - onehot
    ranking = lax.optimization_barrier(jnp.sum(before * onehot, axis=2)).reshape(TOKEN_COUNT, TOPK).astype(jnp.int32)
    block_index = (jnp.arange(TOKEN_COUNT, dtype=jnp.int32) // ROWS).astype(jnp.int32)
    copies = jnp.broadcast_to(normed[:, None, :], (TOKEN_COUNT, TOPK, D))
    buffer = jnp.zeros((blocks, EXPERTS, CAP, D), jnp.bfloat16).at[block_index[:, None], expert_ids, ranking].set(copies)
    per_expert = jnp.transpose(buffer, (1, 0, 2, 3)).reshape(EXPERTS, blocks * CAP, D)

    def run_expert(pieces):
        expert_rows, up_matrix, down_matrix = pieces
        hidden = jax.nn.silu(jnp.dot(expert_rows, up_matrix, preferred_element_type=jnp.float32)).astype(jnp.bfloat16)

        def add_block(running, block_number):
            hidden_part = lax.dynamic_slice_in_dim(hidden, block_number * FFL, FFL, 1)
            down_part = lax.dynamic_slice_in_dim(down_matrix, block_number * FFL, FFL, 0)
            block_sum = lax.optimization_barrier(jnp.dot(hidden_part, down_part, preferred_element_type=jnp.float32).astype(jnp.bfloat16))
            return (running + block_sum.astype(jnp.float32), None)
        running, unused = lax.scan(add_block, jnp.zeros((expert_rows.shape[0], D), jnp.float32), jnp.arange(N_CTX, dtype=jnp.int32))
        return running.astype(jnp.bfloat16)
    outputs = lax.map(run_expert, (per_expert, up_weight, down_weight)).reshape(EXPERTS, blocks, CAP, D)
    picked = outputs[expert_ids, block_index[:, None], ranking].astype(jnp.float32)
    gate_weights = gate_codes.astype(jnp.float32)
    gate_weights = gate_weights / lax.optimization_barrier(jnp.sum(gate_weights, axis=1, keepdims=True))
    mixture_out = lax.optimization_barrier(jnp.sum(gate_weights[:, :, None] * picked, axis=1))
    return (stream_wide + mixture_out).astype(jnp.bfloat16)
```

```python
import functools
import math
import jax
import jax.numpy as jnp
from jax import lax
from jax.experimental import pallas as pl
from jax.experimental.pallas import tpu as pltpu
from jax.sharding import PartitionSpec as P

F32 = jnp.float32
BF16 = jnp.bfloat16
SIDE_X, SIDE_Y = 4, 4
DEPTH, CORES = 8, 2
GROUP = 8
VMEM = pl.BlockSpec(memory_space=pltpu.VMEM)
SMEM = pl.BlockSpec(memory_space=pltpu.SMEM)


def shifted(array, axis, by):
    count = lax.axis_size(axis)
    pairs = [(i, i + by) for i in range(count) if 0 <= i + by < count]
    return lax.ppermute(array, axis, pairs)


def along_plane(array, dx, dy):
    pairs = [
        (x * SIDE_Y + y, (x + dx) % SIDE_X * SIDE_Y + (y + dy) % SIDE_Y)
        for x in range(SIDE_X)
        for y in range(SIDE_Y)
    ]
    return lax.ppermute(array, "ctx", pairs)


def along_depth(array, dz, dc):
    pairs = [
        (z * CORES + c, (z + dz) % DEPTH * CORES + (c + dc) % CORES)
        for z in range(DEPTH)
        for c in range(CORES)
    ]
    return lax.ppermute(array, "exp", pairs)


def silu(v):
    return v / (1.0 + jnp.exp(-v))


def prepare_kernel(inner_ref, border_ref, taps_ref, bias_ref, proj_ref, signal_ref, maps_ref, padded):
    length = inner_ref.shape[0]
    count = taps_ref.shape[0]
    padded[0:8, :] = jnp.zeros((8, padded.shape[1]), F32)
    padded[8 - count + 1 : 8, :] = border_ref[...].astype(F32)
    padded[8:, :] = inner_ref[...].astype(F32)
    total = taps_ref[0:1, :] * padded[8 - count + 1 : 8 - count + 1 + length, :]
    for k in range(1, count):
        start = 8 - count + 1 + k
        total = total + taps_ref[k : k + 1, :] * padded[start : start + length, :]
    signal = silu(total + bias_ref[...])
    signal_ref[...] = signal
    maps_ref[...] = lax.dot_general(
        proj_ref[...],
        signal.astype(BF16),
        (((0,), (1,)), ((), ())),
        preferred_element_type=F32,
    )


def recur(maps_ref, codes_ref, signal_ref, rates, state, out_ref):
    width = codes_ref.shape[1]
    count = rates.shape[0]
    tiles = width // 128

    def group(g, state):
        rows = pl.ds(pl.multiple_of(g * GROUP, GROUP), GROUP)
        codes = codes_ref[rows, :].astype(F32)
        drive = jnp.minimum(codes * (1.0 / 256.0), 1.0) * signal_ref[rows, :]
        lanes = maps_ref.shape[1]
        maps = pltpu.roll(maps_ref[...], (lanes - g * GROUP) % lanes, 1)
        outs = []
        for k in range(GROUP):
            into = jnp.broadcast_to(maps[:count, k : k + 1], (count, 128))
            if out_ref is not None:
                out_of = jnp.broadcast_to(maps[count:, k : k + 1], (count, 128))
            pieces = []
            new = []
            for i in range(tiles):
                cols = slice(i * 128, (i + 1) * 128)
                decay = jnp.exp2(codes[k : k + 1, cols] * rates[:, cols])
                now = decay * state[i] + into * drive[k : k + 1, cols]
                new.append(now)
                if out_ref is not None:
                    pieces.append(jnp.sum(out_of * now, axis=0, keepdims=True))
            state = tuple(new)
            if out_ref is not None:
                outs.append(jnp.concatenate(pieces, axis=1))
        if out_ref is not None:
            out_ref[rows, :] = jnp.concatenate(outs, axis=0)
        return state

    return lax.fori_loop(0, codes_ref.shape[0] // GROUP, group, state)


def end_kernel(parts_ref, codes_ref, signal_ref, rates_ref, maps_ref, sent_ref):
    maps = parts_ref[0]
    for i in range(1, parts_ref.shape[0]):
        maps = maps + parts_ref[i]
    maps_ref[...] = maps
    rates = rates_ref[...] * (-math.log2(math.e) / 256.0)
    count, width = rates.shape
    zero = tuple(jnp.zeros((count, 128), F32) for _ in range(width // 128))
    state = jnp.concatenate(recur(maps_ref, codes_ref, signal_ref, rates, zero, None), axis=1)
    total = jnp.sum(codes_ref[...].astype(F32), axis=0, keepdims=True)
    rows = lax.broadcasted_iota(jnp.int32, (count, width), 0)
    packed = jnp.zeros((count, width), F32)
    for i in range(3):
        part = total.astype(BF16).astype(F32)
        packed = jnp.where(rows == i, part, packed)
        total = total - part
    sent_ref[...] = jnp.concatenate([state, packed], axis=0).astype(BF16)


def scan_kernel(
    where_ref, ends_ref, maps_ref, codes_ref, signal_ref, rates_ref, skip_ref, gate_ref, gated_ref, out
):
    rates = rates_ref[...] * (-math.log2(math.e) / 256.0)
    count, width = rates.shape

    def hop(j, state):
        block = ends_ref[j].astype(F32)
        total = block[count : count + 1] + block[count + 1 : count + 2] + block[count + 2 : count + 3]
        return jnp.exp2(total * rates) * state + block[:count]

    start = lax.fori_loop(0, where_ref[0], hop, jnp.zeros((count, width), F32))
    state = tuple(start[:, i * 128 : (i + 1) * 128] for i in range(width // 128))
    recur(maps_ref, codes_ref, signal_ref, rates, state, out)
    z, c = where_ref[1], where_ref[2]

    def gate(j, carry):
        rows = pl.ds(pl.multiple_of(j * GROUP, GROUP), GROUP)
        to = (j % CORES + CORES - c) % CORES * DEPTH + (j // CORES + DEPTH - z) % DEPTH
        value = out[rows, :] + skip_ref[...] * signal_ref[rows, :]
        gated_ref[pl.ds(pl.multiple_of(to * GROUP, GROUP), GROUP), :] = value * silu(
            gate_ref[rows, :].astype(F32)
        )
        return carry

    lax.fori_loop(0, codes_ref.shape[0] // GROUP, gate, 0)


def state_space(inner_input, gate_input, step_codes, conv_weight, conv_bias, decay_rates, skip_gain, state_proj):
    length, width = inner_input.shape
    taps = conv_weight.shape[0]
    count = decay_rates.shape[0]
    border = shifted(inner_input[length - taps + 1 :], "ctx", 1)
    signal, part = pl.pallas_call(
        prepare_kernel,
        out_shape=(
            jax.ShapeDtypeStruct((length, width), F32),
            jax.ShapeDtypeStruct((2 * count, length), F32),
        ),
        in_specs=[VMEM] * 5,
        out_specs=(VMEM, VMEM),
        scratch_shapes=[pltpu.VMEM((length + 8, width), F32)],
        name="prepare",
    )(inner_input, border, conv_weight, conv_bias[None], state_proj)
    parts = lax.all_gather(part, "exp")
    maps, sent = pl.pallas_call(
        end_kernel,
        out_shape=(
            jax.ShapeDtypeStruct((2 * count, length), F32),
            jax.ShapeDtypeStruct((2 * count, width), BF16),
        ),
        in_specs=[VMEM] * 4,
        out_specs=(VMEM, VMEM),
        name="end_state",
    )(parts, step_codes, signal, decay_rates)
    ends = lax.all_gather(sent, "ctx")
    exp = lax.axis_index("exp")
    where = jnp.stack([lax.axis_index("ctx"), exp // CORES, exp % CORES]).astype(jnp.int32)
    return pl.pallas_call(
        scan_kernel,
        out_shape=jax.ShapeDtypeStruct((length, width), F32),
        in_specs=[SMEM] + [VMEM] * 7,
        out_specs=VMEM,
        scratch_shapes=[pltpu.VMEM((length, width), F32)],
        name="scan",
    )(where, ends, maps, step_codes, signal, decay_rates, skip_gain[None], gate_input)


def project_out(gated, out_proj):
    half = gated.shape[0] // CORES

    def product(rows):
        return jnp.dot(rows.astype(BF16), out_proj, preferred_element_type=F32).astype(BF16)

    theirs = along_depth(product(gated[half:]), 0, 1)
    pair = (product(gated[:half]).astype(F32) + theirs.astype(F32)).astype(BF16)
    blocks = pair.reshape(DEPTH, GROUP, -1)
    total = blocks[0].astype(F32)
    for dz in range(1, DEPTH):
        total = total + along_depth(blocks[dz], dz, 0).astype(F32)
    return total


def sum_side(blocks, dx, dy):
    half = blocks[2].shape[0] // 2
    up = along_plane(blocks[2][:half], dx, dy).astype(F32)
    down = along_plane(blocks[2][half:], -dx, -dy).astype(F32)
    one, three = blocks[1].astype(F32), blocks[3].astype(F32)
    one = jnp.concatenate([one[:half] + up, one[half:]]).astype(BF16)
    three = jnp.concatenate([three[:half], three[half:] + down]).astype(BF16)
    one = along_plane(one, dx, dy)
    three = along_plane(three, -dx, -dy)
    return (blocks[0].astype(F32) + one.astype(F32) + three.astype(F32)).astype(BF16)


def shards(
    inner_input,
    gate_input,
    step_codes,
    conv_weight,
    conv_bias,
    decay_rates,
    skip_gain,
    state_proj,
    out_proj,
    residual,
    norm_gain,
    expert_ids,
    gate_codes,
    up_weight,
    down_weight,
):
    gated = state_space(
        inner_input, gate_input, step_codes, conv_weight, conv_bias, decay_rates, skip_gain, state_proj
    )
    row_count = residual.shape[0]
    mamba_out = project_out(gated, out_proj)
    stream = (residual.astype(F32) + mamba_out).astype(BF16)
    stream_wide = stream.astype(F32)
    normed = (
        stream_wide
        * lax.rsqrt(jnp.mean(stream_wide * stream_wide, axis=-1, keepdims=True) + 1e-05)
        * norm_gain
    ).astype(BF16)
    experts = lax.axis_size("exp") * up_weight.shape[0]
    top_count = expert_ids.shape[1]
    capacity = max(2, 4 * row_count // experts)
    onehot = (
        (expert_ids[:, :, None] == jnp.arange(experts)[None, None, :])
        .astype(jnp.int32)
        .reshape(row_count * top_count, experts)
    )
    before = jnp.cumsum(onehot, axis=0) - onehot
    ranking = jnp.sum(before * onehot, axis=1).reshape(row_count, top_count)
    slot_index = expert_ids * capacity + ranking
    slots = slot_index[:, :, None] == jnp.arange(experts * capacity)[None, None, :]
    dispatch_table = jnp.any(slots, axis=1).astype(BF16)
    up_local = up_weight[0]
    down_local = down_weight[0]
    outgoing = lax.dot_general(
        dispatch_table, normed, (((0,), (0,)), ((), ())), preferred_element_type=F32
    ).astype(BF16)
    arrived = lax.all_to_all(outgoing, "exp", split_axis=0, concat_axis=0, tiled=True)
    segment = lax.all_gather(arrived, "ctx", axis=0, tiled=True)
    hidden = jax.nn.silu(jnp.dot(segment, up_local, preferred_element_type=F32)).astype(BF16)
    partial = jnp.dot(hidden, down_local, preferred_element_type=F32).astype(BF16)
    expert_out = lax.psum_scatter(partial, "ctx", scatter_dimension=0, tiled=True)
    returned = lax.all_to_all(expert_out, "exp", split_axis=0, concat_axis=0, tiled=True)
    gate_weights = gate_codes.astype(F32)
    gate_weights = gate_weights / jnp.sum(gate_weights, axis=1, keepdims=True)
    picked = jnp.take(returned, slot_index, axis=0).astype(F32)
    mixture_out = jnp.sum(gate_weights[:, :, None] * picked, axis=1)
    return (stream_wide + mixture_out).astype(BF16)


def solution(mesh):
    return jax.shard_map(
        shards,
        mesh=mesh,
        in_specs=(
            P("ctx", "exp"),
            P("ctx", "exp"),
            P("ctx", "exp"),
            P(None, "exp"),
            P("exp"),
            P(None, "exp"),
            P("exp"),
            P("exp", None),
            P("exp", None),
            P(("ctx", "exp"), None),
            P(),
            P(("ctx", "exp"), None),
            P(("ctx", "exp"), None),
            P("exp", None, "ctx"),
            P("exp", "ctx", None),
        ),
        out_specs=P(("ctx", "exp"), None),
        check_vma=False,
    )
```

```python
import functools
import math
import jax
import jax.numpy as jnp
from jax import lax
from jax.experimental import pallas as pl
from jax.experimental.pallas import tpu as pltpu
from jax.sharding import PartitionSpec as P

F32 = jnp.float32
BF16 = jnp.bfloat16
SIDE_X, SIDE_Y = 4, 4
DEPTH, CORES = 8, 2
GROUP = 8
VMEM = pl.BlockSpec(memory_space=pltpu.VMEM)
SMEM = pl.BlockSpec(memory_space=pltpu.SMEM)


def shifted(array, axis, by):
    count = lax.axis_size(axis)
    pairs = [(i, i + by) for i in range(count) if 0 <= i + by < count]
    return lax.ppermute(array, axis, pairs)


def along_plane(array, dx, dy):
    pairs = [
        (x * SIDE_Y + y, (x + dx) % SIDE_X * SIDE_Y + (y + dy) % SIDE_Y)
        for x in range(SIDE_X)
        for y in range(SIDE_Y)
    ]
    return lax.ppermute(array, "ctx", pairs)


def along_depth(array, target):
    pairs = []
    for z in range(DEPTH):
        for c in range(CORES):
            to_z, to_c = target(z, c)
            pairs.append((z * CORES + c, to_z % DEPTH * CORES + to_c))
    return lax.ppermute(array, "exp", pairs)


def near(array):
    return [
        along_depth(array, lambda z, c: (z, 1 - c)),
        along_depth(array, lambda z, c: (z ^ 1, c)),
        along_depth(array, lambda z, c: (z ^ 1, 1 - c)),
    ]


def far(arrays):
    return [along_depth(a, lambda z, c, k=k: (z + 2 * k, c)) for k, a in enumerate(arrays) if k]


def silu(v):
    return v / (1.0 + jnp.exp(-v))


def prepare_kernel(inner_ref, border_ref, taps_ref, bias_ref, proj_ref, signal_ref, maps_ref, padded):
    length = inner_ref.shape[0]
    count = taps_ref.shape[0]
    padded[0:8, :] = jnp.zeros((8, padded.shape[1]), F32)
    padded[8 - count + 1 : 8, :] = border_ref[...].astype(F32)
    padded[8:, :] = inner_ref[...].astype(F32)
    total = taps_ref[0:1, :] * padded[8 - count + 1 : 8 - count + 1 + length, :]
    for k in range(1, count):
        start = 8 - count + 1 + k
        total = total + taps_ref[k : k + 1, :] * padded[start : start + length, :]
    signal = silu(total + bias_ref[...])
    signal_ref[...] = signal
    maps_ref[...] = lax.dot_general(
        proj_ref[...],
        signal.astype(BF16),
        (((1,), (1,)), ((), ())),
        preferred_element_type=F32,
    )


def recur(maps_ref, codes_ref, signal_ref, rates, state, out_ref):
    width = codes_ref.shape[1]
    count = rates.shape[0]
    tiles = width // 128

    def group(g, state):
        rows = pl.ds(pl.multiple_of(g * GROUP, GROUP), GROUP)
        codes = codes_ref[rows, :].astype(F32)
        drive = jnp.minimum(codes * (1.0 / 256.0), 1.0) * signal_ref[rows, :]
        lanes = maps_ref.shape[1]
        maps = pltpu.roll(maps_ref[...], (lanes - g * GROUP) % lanes, 1)
        outs = []
        for k in range(GROUP):
            into = jnp.broadcast_to(maps[:count, k : k + 1], (count, 128))
            if out_ref is not None:
                out_of = jnp.broadcast_to(maps[count:, k : k + 1], (count, 128))
            pieces = []
            new = []
            for i in range(tiles):
                cols = slice(i * 128, (i + 1) * 128)
                decay = jnp.exp2(codes[k : k + 1, cols] * rates[:, cols])
                now = decay * state[i] + into * drive[k : k + 1, cols]
                new.append(now)
                if out_ref is not None:
                    pieces.append(jnp.sum(out_of * now, axis=0, keepdims=True))
            state = tuple(new)
            if out_ref is not None:
                outs.append(jnp.concatenate(pieces, axis=1))
        if out_ref is not None:
            out_ref[rows, :] = jnp.concatenate(outs, axis=0)
        return state

    return lax.fori_loop(0, codes_ref.shape[0] // GROUP, group, state)


def end_kernel(a_ref, b_ref, c_ref, d_ref, codes_ref, signal_ref, rates_ref, maps_ref, sent_ref):
    maps_ref[...] = (a_ref[...] + b_ref[...]) + (c_ref[...] + d_ref[...])
    rates = rates_ref[...] * (-math.log2(math.e) / 256.0)
    count, width = rates.shape
    zero = tuple(jnp.zeros((count, 128), F32) for _ in range(width // 128))
    state = jnp.concatenate(recur(maps_ref, codes_ref, signal_ref, rates, zero, None), axis=1)
    total = jnp.sum(codes_ref[...].astype(F32), axis=0, keepdims=True)
    rows = lax.broadcasted_iota(jnp.int32, (count, width), 0)
    packed = jnp.zeros((count, width), F32)
    for i in range(3):
        part = total.astype(BF16).astype(F32)
        packed = jnp.where(rows == i, part, packed)
        total = total - part
    sent_ref[...] = jnp.concatenate([state, packed], axis=0).astype(BF16)


def scan_kernel(
    where_ref, ends_ref, maps_ref, codes_ref, signal_ref, rates_ref, skip_ref, gate_ref, gated_ref, out, arranged
):
    rates = rates_ref[...] * (-math.log2(math.e) / 256.0)
    count, width = rates.shape

    x, y = where_ref[0] // SIDE_Y, where_ref[0] % SIDE_Y

    def hop(j, state):
        at = (x + SIDE_X - j // SIDE_Y) % SIDE_X * SIDE_Y + (y + SIDE_Y - j % SIDE_Y) % SIDE_Y
        block = ends_ref[pl.ds(pl.multiple_of(at * 2 * count, 2 * count), 2 * count), :].astype(F32)
        total = block[count : count + 1] + block[count + 1 : count + 2] + block[count + 2 : count + 3]
        return jnp.exp2(total * rates) * state + block[:count]

    start = lax.fori_loop(0, where_ref[0], hop, jnp.zeros((count, width), F32))
    state = tuple(start[:, i * 128 : (i + 1) * 128] for i in range(width // 128))
    recur(maps_ref, codes_ref, signal_ref, rates, state, out)
    z, c = where_ref[1], where_ref[2]
    pairs = DEPTH // 2

    def gate(j, carry):
        rows = pl.ds(pl.multiple_of(j * GROUP, GROUP), GROUP)
        to_z, to_c = j // CORES, j % CORES
        to = ((to_c + c) % 2 * 2 + (to_z + z) % 2) * pairs + (to_z // 2 + pairs - z // 2) % pairs
        value = out[rows, :] + skip_ref[...] * signal_ref[rows, :]
        arranged[pl.ds(pl.multiple_of(to * GROUP, GROUP), GROUP), :] = value * silu(
            gate_ref[rows, :].astype(F32)
        )
        return carry

    lax.fori_loop(0, codes_ref.shape[0] // GROUP, gate, 0)
    gated_ref[...] = arranged[...].astype(BF16)


def state_space(inner_input, gate_input, step_codes, conv_weight, conv_bias, decay_rates, skip_gain, state_proj):
    length, width = inner_input.shape
    taps = conv_weight.shape[0]
    count = decay_rates.shape[0]
    border = shifted(inner_input[length - taps + 1 :], "ctx", 1)
    signal, part = pl.pallas_call(
        prepare_kernel,
        out_shape=(
            jax.ShapeDtypeStruct((length, width), F32),
            jax.ShapeDtypeStruct((2 * count, length), F32),
        ),
        in_specs=[VMEM] * 5,
        out_specs=(VMEM, VMEM),
        scratch_shapes=[pltpu.VMEM((length + 8, width), F32)],
        name="prepare",
    )(inner_input, border, conv_weight, conv_bias[None], state_proj.T)
    part = sum(near(part), part)
    maps, sent = pl.pallas_call(
        end_kernel,
        out_shape=(
            jax.ShapeDtypeStruct((2 * count, length), F32),
            jax.ShapeDtypeStruct((2 * count, width), BF16),
        ),
        in_specs=[VMEM] * 7,
        out_specs=(VMEM, VMEM),
        name="end_state",
    )(part, *far([part] * (DEPTH // 2)), step_codes, signal, decay_rates)
    ends = jnp.concatenate([sent] + [along_plane(sent, 0, k) for k in range(1, SIDE_Y)])
    ends = jnp.concatenate([ends] + [along_plane(ends, k, 0) for k in range(1, SIDE_X)])
    exp = lax.axis_index("exp")
    where = jnp.stack([lax.axis_index("ctx"), exp // CORES, exp % CORES]).astype(jnp.int32)
    return pl.pallas_call(
        scan_kernel,
        out_shape=jax.ShapeDtypeStruct((length, width), BF16),
        in_specs=[SMEM] + [VMEM] * 7,
        out_specs=VMEM,
        scratch_shapes=[pltpu.VMEM((length, width), F32)] * 2,
        name="scan",
    )(where, ends, maps, step_codes, signal, decay_rates, skip_gain[None], gate_input)


def added(*arrays):
    return sum(a.astype(F32) for a in arrays).astype(BF16)


def project_out(gated, out_proj):
    product = jnp.dot(gated, out_proj, preferred_element_type=F32).astype(BF16)
    half = product.shape[0] // 2
    pair = added(product[:half], along_depth(product[half:], lambda z, c: (z, 1 - c)))
    half = half // 2
    chip = added(pair[:half], along_depth(pair[half:], lambda z, c: (z ^ 1, c)))
    blocks = [chip[k * GROUP : (k + 1) * GROUP] for k in range(DEPTH // 2)]
    return sum((a.astype(F32) for a in far(blocks)), blocks[0].astype(F32))


def expert(rows, up, down):
    hidden = jax.nn.silu(jnp.dot(rows, up, preferred_element_type=F32)).astype(BF16)
    return jnp.dot(hidden, down, preferred_element_type=F32).astype(BF16)


def split(array, parts):
    size = array.shape[0] // parts
    return [array[k * size : (k + 1) * size] for k in range(parts)]


def run_expert(arrived, up, down):
    sides = ((1, 0), (0, 1))
    steps = (1, 2, 3)
    gathered = []
    for (dx, dy), rows in zip(sides, split(arrived, 2)):
        gathered.append(jnp.concatenate([rows] + [along_plane(rows, k * dx, k * dy) for k in steps]))
    after, before = [], []
    for (dy, dx), rows in zip(sides, gathered):
        after.append(along_plane(rows, dx, dy))
        before.append(along_plane(rows, -dx, -dy))
    after, before = lax.optimization_barrier((after, before))
    opposite = []
    for (dy, dx), a, b in zip(sides, after, before):
        half = a.shape[0] // 2
        opposite += [along_plane(a[:half], dx, dy), along_plane(b[half:], -dx, -dy)]
    near_by = split(expert(jnp.concatenate(gathered + after + before), up, down), 6)
    far_off = split(expert(jnp.concatenate(opposite), up, down), 4)
    passed = []
    for i, (dy, dx) in enumerate(sides):
        passed.append(along_plane(far_off[2 * i], -dx, -dy))
        passed.append(along_plane(far_off[2 * i + 1], dx, dy))
    passed = lax.optimization_barrier(passed)
    sums = []
    for i, (dy, dx) in enumerate(sides):
        to_after, to_before = near_by[2 + i], near_by[4 + i]
        half = to_after.shape[0] // 2
        one = jnp.concatenate([added(to_after[:half], passed[2 * i]), to_after[half:]])
        three = jnp.concatenate([to_before[:half], added(to_before[half:], passed[2 * i + 1])])
        sums.append(added(near_by[i], along_plane(one, -dx, -dy), along_plane(three, dx, dy)))
    result = []
    for (dx, dy), total in zip(sides, sums):
        blocks = split(total, 4)
        result.append(added(blocks[0], *[along_plane(blocks[k], -k * dx, -k * dy) for k in steps]))
    return jnp.concatenate(result)


def shards(
    inner_input,
    gate_input,
    step_codes,
    conv_weight,
    conv_bias,
    decay_rates,
    skip_gain,
    state_proj,
    out_proj,
    residual,
    norm_gain,
    expert_ids,
    gate_codes,
    up_weight,
    down_weight,
):
    gated = state_space(
        inner_input, gate_input, step_codes, conv_weight, conv_bias, decay_rates, skip_gain, state_proj
    )
    row_count = residual.shape[0]
    mamba_out = project_out(gated, out_proj)
    stream = (residual.astype(F32) + mamba_out).astype(BF16)
    stream_wide = stream.astype(F32)
    normed = (
        stream_wide
        * lax.rsqrt(jnp.mean(stream_wide * stream_wide, axis=-1, keepdims=True) + 1e-05)
        * norm_gain
    ).astype(BF16)
    experts = lax.axis_size("exp") * up_weight.shape[0]
    top_count = expert_ids.shape[1]
    capacity = max(2, 4 * row_count // experts)
    onehot = (
        (expert_ids[:, :, None] == jnp.arange(experts)[None, None, :])
        .astype(jnp.int32)
        .reshape(row_count * top_count, experts)
    )
    before = jnp.cumsum(onehot, axis=0) - onehot
    ranking = jnp.sum(before * onehot, axis=1).reshape(row_count, top_count)
    slot_index = expert_ids * capacity + ranking
    slots = slot_index[:, :, None] == jnp.arange(experts * capacity)[None, None, :]
    dispatch_table = jnp.any(slots, axis=1).astype(BF16)
    up_local = up_weight[0]
    down_local = down_weight[0]
    outgoing = lax.dot_general(
        dispatch_table, normed, (((0,), (0,)), ((), ())), preferred_element_type=F32
    ).astype(BF16)
    arrived = lax.all_to_all(outgoing, "exp", split_axis=0, concat_axis=0, tiled=True)
    expert_out = run_expert(arrived, up_local, down_local)
    returned = lax.all_to_all(expert_out, "exp", split_axis=0, concat_axis=0, tiled=True)
    gate_weights = gate_codes.astype(F32)
    gate_weights = gate_weights / jnp.sum(gate_weights, axis=1, keepdims=True)
    picked = jnp.take(returned, slot_index, axis=0).astype(F32)
    mixture_out = jnp.sum(gate_weights[:, :, None] * picked, axis=1)
    return (stream_wide + mixture_out).astype(BF16)


def solution(mesh):
    return jax.shard_map(
        shards,
        mesh=mesh,
        in_specs=(
            P("ctx", "exp"),
            P("ctx", "exp"),
            P("ctx", "exp"),
            P(None, "exp"),
            P("exp"),
            P(None, "exp"),
            P("exp"),
            P("exp", None),
            P("exp", None),
            P(("ctx", "exp"), None),
            P(),
            P(("ctx", "exp"), None),
            P(("ctx", "exp"), None),
            P("exp", None, "ctx"),
            P("exp", "ctx", None),
        ),
        out_specs=P(("ctx", "exp"), None),
        check_vma=False,
    )
```

```python
import functools
import math
import jax
import jax.numpy as jnp
from jax import lax
from jax.experimental import pallas as pl
from jax.experimental.pallas import tpu as pltpu
from jax.sharding import PartitionSpec as P

F32 = jnp.float32
BF16 = jnp.bfloat16
SIDE_X, SIDE_Y = 4, 4
DEPTH, CORES = 8, 2
GROUP = 8
VMEM = pl.BlockSpec(memory_space=pltpu.VMEM)
HBM = pl.BlockSpec(memory_space=pltpu.HBM)
SMALL = pltpu.CompilerParams(vmem_limit_bytes=8 * 1024 * 1024)
MEDIUM = pltpu.CompilerParams(vmem_limit_bytes=20 * 1024 * 1024)


def shifted(array, axis, by):
    count = lax.axis_size(axis)
    pairs = [(i, i + by) for i in range(count) if 0 <= i + by < count]
    return lax.ppermute(array, axis, pairs)


def along_plane(array, dx, dy):
    pairs = [
        (x * SIDE_Y + y, (x + dx) % SIDE_X * SIDE_Y + (y + dy) % SIDE_Y)
        for x in range(SIDE_X)
        for y in range(SIDE_Y)
    ]
    return lax.ppermute(array, "ctx", pairs)


def along_depth(array, target):
    pairs = []
    for z in range(DEPTH):
        for c in range(CORES):
            to_z, to_c = target(z, c)
            pairs.append((z * CORES + c, to_z % DEPTH * CORES + to_c))
    return lax.ppermute(array, "exp", pairs)


def near(array):
    return [
        along_depth(array, lambda z, c: (z, 1 - c)),
        along_depth(array, lambda z, c: (z ^ 1, c)),
        along_depth(array, lambda z, c: (z ^ 1, 1 - c)),
    ]


def far(arrays):
    return [along_depth(a, lambda z, c, k=k: (z + 2 * k, c)) for k, a in enumerate(arrays) if k]


def silu(v):
    return v / (1.0 + jnp.exp(-v))


def stage_kernel(
    inner_ref, codes_ref, gate_ref, taps_ref, bias_ref, proj_ref, rates_ref, skip_ref,
    conv_out, codes_out, gate_out, taps_out, proj_out, rates_out, skip_out,
    inner, codes, gate, bias, rates, padded, sems,
):
    moves = [
        (inner_ref, inner),
        (taps_ref, taps_out),
        (bias_ref, bias),
        (codes_ref, codes),
        (gate_ref, gate),
        (proj_ref, proj_out),
        (rates_ref, rates),
        (skip_ref, skip_out),
    ]
    copies = [pltpu.make_async_copy(a, b, sems.at[k]) for k, (a, b) in enumerate(moves)]
    for copy in copies:
        copy.start()
    length = inner.shape[0]
    count = taps_out.shape[0]
    padded[0:8, :] = jnp.zeros((8, padded.shape[1]), F32)
    for copy in copies[:3]:
        copy.wait()
    padded[8:, :] = inner[...].astype(F32)
    total = taps_out[0:1, :] * padded[8 - count + 1 : 8 - count + 1 + length, :]
    for k in range(1, count):
        start = 8 - count + 1 + k
        total = total + taps_out[k : k + 1, :] * padded[start : start + length, :]
    conv_out[...] = total + bias[...]
    for copy in copies[3:]:
        copy.wait()
    codes_out[...] = codes[...].astype(F32)
    gate_out[...] = silu(gate[...].astype(F32))
    rates_out[...] = rates[...] * (-math.log2(math.e) / 256.0)


def signal_kernel(border_ref, conv_ref, codes_ref, taps_ref, proj_ref, signal_ref, drive_ref, maps_ref):
    count = taps_ref.shape[0]
    width = conv_ref.shape[1]
    border = border_ref[...].astype(F32)
    rows = lax.broadcasted_iota(jnp.int32, (8, width), 0)
    first = jnp.zeros((8, width), F32)
    for t in range(count - 1):
        row = jnp.zeros((1, width), F32)
        for k in range(count - 1 - t):
            row = row + taps_ref[k : k + 1, :] * border[t + k : t + k + 1, :]
        first = jnp.where(rows == t, row, first)
    signal_ref[...] = silu(conv_ref[...])
    signal_ref[0:8, :] = silu(conv_ref[0:8, :] + first)
    signal = signal_ref[...]
    drive_ref[...] = jnp.minimum(codes_ref[...] * (1.0 / 256.0), 1.0) * signal
    maps_ref[...] = lax.dot_general(
        proj_ref[...],
        signal.astype(BF16),
        (((1,), (1,)), ((), ())),
        preferred_element_type=F32,
    )


def recur(maps_ref, codes_ref, drive_ref, rates, state, out_ref):
    width = codes_ref.shape[1]
    count = rates.shape[0]
    tiles = width // 128

    def group(g, state):
        rows = pl.ds(pl.multiple_of(g * GROUP, GROUP), GROUP)
        codes = codes_ref[rows, :]
        drive = drive_ref[rows, :]
        lanes = maps_ref.shape[1]
        maps = pltpu.roll(maps_ref[...], (lanes - g * GROUP) % lanes, 1)
        outs = []
        for k in range(GROUP):
            into = jnp.broadcast_to(maps[:count, k : k + 1], (count, 128))
            if out_ref is not None:
                out_of = jnp.broadcast_to(maps[count:, k : k + 1], (count, 128))
            pieces = []
            new = []
            for i in range(tiles):
                cols = slice(i * 128, (i + 1) * 128)
                decay = jnp.exp2(codes[k : k + 1, cols] * rates[:, cols])
                now = decay * state[i] + into * drive[k : k + 1, cols]
                new.append(now)
                if out_ref is not None:
                    pieces.append(jnp.sum(out_of * now, axis=0, keepdims=True))
            state = tuple(new)
            if out_ref is not None:
                outs.append(jnp.concatenate(pieces, axis=1))
        if out_ref is not None:
            out_ref[rows, :] = jnp.concatenate(outs, axis=0)
        return state

    return lax.fori_loop(0, codes_ref.shape[0] // GROUP, group, state)


def end_kernel(a_ref, b_ref, c_ref, d_ref, codes_ref, drive_ref, rates_ref, maps_ref, sent_ref):
    maps_ref[...] = (a_ref[...] + b_ref[...]) + (c_ref[...] + d_ref[...])
    rates = rates_ref[...]
    count, width = rates.shape
    zero = tuple(jnp.zeros((count, 128), F32) for _ in range(width // 128))
    state = jnp.concatenate(recur(maps_ref, codes_ref, drive_ref, rates, zero, None), axis=1)
    total = jnp.sum(codes_ref[...], axis=0, keepdims=True)
    rows = lax.broadcasted_iota(jnp.int32, (count, width), 0)
    packed = jnp.zeros((count, width), F32)
    for i in range(3):
        part = total.astype(BF16).astype(F32)
        packed = jnp.where(rows == i, part, packed)
        total = total - part
    sent_ref[...] = jnp.concatenate([state, packed], axis=0).astype(BF16)


def scan_kernel(
    ends_ref, maps_ref, codes_ref, drive_ref, signal_ref, rates_ref, skip_ref, gate_ref, proj_ref,
    own_ref, other_ref, out, arranged, gated, proj, sem,
):
    fetch = pltpu.make_async_copy(proj_ref, proj, sem)
    fetch.start()
    rates = rates_ref[...]
    count, width = rates.shape
    ctx, exp = lax.axis_index("ctx"), lax.axis_index("exp")
    x, y = ctx // SIDE_Y, ctx % SIDE_Y

    def hop(j, state):
        at = (x + SIDE_X - j // SIDE_Y) % SIDE_X * SIDE_Y + (y + SIDE_Y - j % SIDE_Y) % SIDE_Y
        block = ends_ref[pl.ds(pl.multiple_of(at * 2 * count, 2 * count), 2 * count), :].astype(F32)
        total = block[count : count + 1] + block[count + 1 : count + 2] + block[count + 2 : count + 3]
        return jnp.exp2(total * rates) * state + block[:count]

    start = lax.fori_loop(0, ctx, hop, jnp.zeros((count, width), F32))
    state = tuple(start[:, i * 128 : (i + 1) * 128] for i in range(width // 128))
    recur(maps_ref, codes_ref, drive_ref, rates, state, out)
    z, c = exp // CORES, exp % CORES
    pairs = DEPTH // 2

    def gate(j, carry):
        rows = pl.ds(pl.multiple_of(j * GROUP, GROUP), GROUP)
        to_z, to_c = j // CORES, j % CORES
        to = ((to_c + c) % 2 * 2 + (to_z + z) % 2) * pairs + (to_z // 2 + pairs - z // 2) % pairs
        value = out[rows, :] + skip_ref[...] * signal_ref[rows, :]
        arranged[pl.ds(pl.multiple_of(to * GROUP, GROUP), GROUP), :] = value * gate_ref[rows, :]
        return carry

    lax.fori_loop(0, codes_ref.shape[0] // GROUP, gate, 0)
    gated[...] = arranged[...].astype(BF16)
    fetch.wait()
    half = own_ref.shape[0]
    step = 512

    def product(k, carry):
        cols = pl.ds(pl.multiple_of(k * step, step), step)
        block = jnp.dot(gated[...], proj[:, cols], preferred_element_type=F32)
        own_ref[:, cols] = block[:half].astype(BF16)
        other_ref[:, cols] = block[half:].astype(BF16)
        return carry

    lax.fori_loop(0, proj.shape[1] // step, product, 0)


def state_space(
    inner_input, gate_input, step_codes, conv_weight, conv_bias, decay_rates, skip_gain, state_proj, out_proj
):
    length, width = inner_input.shape
    taps = conv_weight.shape[0]
    count = decay_rates.shape[0]
    model = out_proj.shape[1]
    border = shifted(inner_input[length - taps + 1 :], "ctx", 1)

    def wide(rows, kind=F32):
        return jax.ShapeDtypeStruct((rows, width), kind)

    maps_shape = jax.ShapeDtypeStruct((2 * count, length), F32)
    conv, codes, gate, taps_in, proj, rates, skip = pl.pallas_call(
        stage_kernel,
        out_shape=(
            wide(length), wide(length), wide(length), wide(taps), wide(2 * count, BF16), wide(count), wide(1),
        ),
        in_specs=[HBM] * 8,
        out_specs=(VMEM,) * 7,
        scratch_shapes=[
            pltpu.VMEM((length, width), BF16),
            pltpu.VMEM((length, width), jnp.int32),
            pltpu.VMEM((length, width), BF16),
            pltpu.VMEM((1, width), F32),
            pltpu.VMEM((count, width), F32),
            pltpu.VMEM((length + 8, width), F32),
            pltpu.SemaphoreType.DMA((8,)),
        ],
        compiler_params=SMALL,
        cost_estimate=pl.CostEstimate(flops=1 << 20, bytes_accessed=8 << 20, transcendentals=1 << 16),
        name="stage",
    )(
        *in_hbm(
            inner_input,
            step_codes,
            gate_input,
            conv_weight,
            conv_bias[None],
            state_proj.T,
            decay_rates,
            skip_gain[None],
        )
    )
    signal, drive, part = pl.pallas_call(
        signal_kernel,
        out_shape=(wide(length), wide(length), maps_shape),
        in_specs=[VMEM] * 5,
        out_specs=(VMEM,) * 3,
        compiler_params=SMALL,
        name="signal",
    )(border, conv, codes, taps_in, proj)
    part = sum(near(part), part)
    maps, sent = pl.pallas_call(
        end_kernel,
        out_shape=(maps_shape, wide(2 * count, BF16)),
        in_specs=[VMEM] * 7,
        out_specs=(VMEM,) * 2,
        compiler_params=SMALL,
        name="end_state",
    )(part, *far([part] * (DEPTH // 2)), codes, drive, rates)
    ends = join([sent] + [along_plane(sent, 0, k) for k in range(1, SIDE_Y)])
    ends = join([ends] + [along_plane(ends, k, 0) for k in range(1, SIDE_X)])
    half = jax.ShapeDtypeStruct((length // 2, model), BF16)
    return pl.pallas_call(
        scan_kernel,
        out_shape=(half, half),
        in_specs=[VMEM] * 8 + [HBM],
        out_specs=(VMEM,) * 2,
        scratch_shapes=[
            pltpu.VMEM((length, width), F32),
            pltpu.VMEM((length, width), F32),
            pltpu.VMEM((length, width), BF16),
            pltpu.VMEM((width, model), BF16),
            pltpu.SemaphoreType.DMA,
        ],
        compiler_params=MEDIUM,
        name="scan",
    )(ends, maps, codes, drive, signal, rates, skip, gate, *in_hbm(out_proj))


def join_kernel(*refs):
    out = refs[-1]
    at = 0
    for ref in refs[:-1]:
        out[at : at + ref.shape[0], :] = ref[...]
        at += ref.shape[0]


def join(arrays):
    rows = sum(a.shape[0] for a in arrays)
    return pl.pallas_call(
        join_kernel,
        out_shape=jax.ShapeDtypeStruct((rows,) + arrays[0].shape[1:], arrays[0].dtype),
        in_specs=[VMEM] * len(arrays),
        out_specs=VMEM,
        compiler_params=SMALL,
        name="join",
    )(*arrays)


def in_hbm(*arrays):
    return [pltpu.with_memory_space_constraint(a, pltpu.HBM) for a in arrays]


def added(*arrays):
    return sum(a.astype(F32) for a in arrays).astype(BF16)


def sum_out(own, other):
    pair = added(own, along_depth(other, lambda z, c: (z, 1 - c)))
    half = pair.shape[0] // 2
    chip = added(pair[:half], along_depth(pair[half:], lambda z, c: (z ^ 1, c)))
    blocks = [chip[k * GROUP : (k + 1) * GROUP] for k in range(DEPTH // 2)]
    return sum((a.astype(F32) for a in far(blocks)), blocks[0].astype(F32))


def expert_kernel(count, *refs):
    pieces, (up_ref, down_ref), outs = refs[:count], refs[count : count + 2], refs[count + 2 : 2 * count + 2]
    rows, hidden, up_in, down_in, sems = refs[2 * count + 2 :]
    step = 256
    fetches = []
    for k in range(up_ref.shape[1] // step):
        cols = pl.ds(k * step, step)
        fetches.append(pltpu.make_async_copy(up_ref.at[:, cols], up_in.at[:, cols], sems.at[k]))
    fetches.append(pltpu.make_async_copy(down_ref, down_in, sems.at[len(fetches)]))
    for fetch in fetches:
        fetch.start()
    places = []
    at = 0
    for ref in pieces:
        places.append(slice(at, at + ref.shape[0]))
        rows[places[-1], :] = ref[...]
        at += ref.shape[0]
    for k, fetch in enumerate(fetches[:-1]):
        fetch.wait()
        cols = slice(k * step, (k + 1) * step)
        block = jnp.dot(rows[...], up_in[:, cols], preferred_element_type=F32)
        hidden[:, cols] = silu(block).astype(BF16)
    fetches[-1].wait()

    def down(k, carry):
        cols = pl.ds(pl.multiple_of(k * step, step), step)
        block = jnp.dot(hidden[...], down_in[:, cols], preferred_element_type=F32).astype(BF16)
        for place, out in zip(places, outs):
            out[:, cols] = block[place]
        return carry

    lax.fori_loop(0, down_in.shape[1] // step, down, 0)


def expert(pieces, up, down):
    size = sum(p.shape[0] for p in pieces)
    model, width = up.shape
    return pl.pallas_call(
        functools.partial(expert_kernel, len(pieces)),
        out_shape=tuple(jax.ShapeDtypeStruct(p.shape, BF16) for p in pieces),
        in_specs=[VMEM] * len(pieces) + [HBM] * 2,
        out_specs=(VMEM,) * len(pieces),
        scratch_shapes=[
            pltpu.VMEM((size, model), BF16),
            pltpu.VMEM((size, width), BF16),
            pltpu.VMEM(up.shape, BF16),
            pltpu.VMEM(down.shape, BF16),
            pltpu.SemaphoreType.DMA((width // 256 + 1,)),
        ],
        compiler_params=MEDIUM,
        cost_estimate=pl.CostEstimate(
            flops=4 * size * model * width, bytes_accessed=4 * size * model, transcendentals=size * width
        ),
        name="expert",
    )(*pieces, *in_hbm(up, down))


def split(array, parts):
    size = array.shape[0] // parts
    return [array[k * size : (k + 1) * size] for k in range(parts)]


def run_expert(arrived, up, down):
    sides = ((1, 0), (0, 1))
    steps = (1, 2, 3)
    gathered = []
    for (dx, dy), rows in zip(sides, split(arrived, 2)):
        gathered.append(join([rows] + [along_plane(rows, k * dx, k * dy) for k in steps]))
    after, before = [], []
    for (dy, dx), rows in zip(sides, gathered):
        after.append(along_plane(rows, dx, dy))
        before.append(along_plane(rows, -dx, -dy))
    after, before = lax.optimization_barrier((after, before))
    opposite = []
    for (dy, dx), a, b in zip(sides, after, before):
        half = a.shape[0] // 2
        opposite += [along_plane(a[:half], dx, dy), along_plane(b[half:], -dx, -dy)]
    close = expert(gathered + after + before, up, down)
    remote = expert(opposite, up, down)
    passed = []
    for i, (dy, dx) in enumerate(sides):
        first, second = remote[2 * i : 2 * i + 2]
        passed += [along_plane(first, -dx, -dy), along_plane(second, dx, dy)]
    passed = lax.optimization_barrier(passed)
    sums = []
    for i, (dy, dx) in enumerate(sides):
        own, to_after, to_before = close[i], close[2 + i], close[4 + i]
        half = to_after.shape[0] // 2
        one = jnp.concatenate([added(to_after[:half], passed[2 * i]), to_after[half:]])
        three = jnp.concatenate([to_before[:half], added(to_before[half:], passed[2 * i + 1])])
        sums.append(added(own, along_plane(one, -dx, -dy), along_plane(three, dx, dy)))
    result = []
    for (dx, dy), total in zip(sides, sums):
        blocks = split(total, 4)
        result.append(added(blocks[0], *[along_plane(blocks[k], -k * dx, -k * dy) for k in steps]))
    return jnp.concatenate(result)


def shards(
    inner_input,
    gate_input,
    step_codes,
    conv_weight,
    conv_bias,
    decay_rates,
    skip_gain,
    state_proj,
    out_proj,
    residual,
    norm_gain,
    expert_ids,
    gate_codes,
    up_weight,
    down_weight,
):
    own, other = state_space(
        inner_input,
        gate_input,
        step_codes,
        conv_weight,
        conv_bias,
        decay_rates,
        skip_gain,
        state_proj,
        out_proj,
    )
    row_count = residual.shape[0]
    mamba_out = sum_out(own, other)
    stream = (residual.astype(F32) + mamba_out).astype(BF16)
    stream_wide = stream.astype(F32)
    normed = (
        stream_wide
        * lax.rsqrt(jnp.mean(stream_wide * stream_wide, axis=-1, keepdims=True) + 1e-05)
        * norm_gain
    ).astype(BF16)
    experts = lax.axis_size("exp") * up_weight.shape[0]
    top_count = expert_ids.shape[1]
    capacity = max(2, 4 * row_count // experts)
    onehot = (
        (expert_ids[:, :, None] == jnp.arange(experts)[None, None, :])
        .astype(jnp.int32)
        .reshape(row_count * top_count, experts)
    )
    before = jnp.cumsum(onehot, axis=0) - onehot
    ranking = jnp.sum(before * onehot, axis=1).reshape(row_count, top_count)
    slot_index = expert_ids * capacity + ranking
    slots = slot_index[:, :, None] == jnp.arange(experts * capacity)[None, None, :]
    dispatch_table = jnp.any(slots, axis=1).astype(BF16)
    up_local = up_weight[0]
    down_local = down_weight[0]
    outgoing = lax.dot_general(
        dispatch_table, normed, (((0,), (0,)), ((), ())), preferred_element_type=F32
    ).astype(BF16)
    arrived = lax.all_to_all(outgoing, "exp", split_axis=0, concat_axis=0, tiled=True)
    expert_out = run_expert(arrived, up_local, down_local)
    returned = lax.all_to_all(expert_out, "exp", split_axis=0, concat_axis=0, tiled=True)
    gate_weights = gate_codes.astype(F32)
    gate_weights = gate_weights / jnp.sum(gate_weights, axis=1, keepdims=True)
    picked = jnp.take(returned, slot_index, axis=0).astype(F32)
    mixture_out = jnp.sum(gate_weights[:, :, None] * picked, axis=1)
    return (stream_wide + mixture_out).astype(BF16)


def solution(mesh):
    return jax.shard_map(
        shards,
        mesh=mesh,
        in_specs=(
            P("ctx", "exp"),
            P("ctx", "exp"),
            P("ctx", "exp"),
            P(None, "exp"),
            P("exp"),
            P(None, "exp"),
            P("exp"),
            P("exp", None),
            P("exp", None),
            P(("ctx", "exp"), None),
            P(),
            P(("ctx", "exp"), None),
            P(("ctx", "exp"), None),
            P("exp", None, "ctx"),
            P("exp", "ctx", None),
        ),
        out_specs=P(("ctx", "exp"), None),
        check_vma=False,
    )
```

```python
import functools
import math
import jax
import jax.numpy as jnp
from jax import lax
from jax.experimental import pallas as pl
from jax.experimental.pallas import tpu as pltpu
from jax.sharding import PartitionSpec as P

F32 = jnp.float32
BF16 = jnp.bfloat16
SIDE_X, SIDE_Y = 4, 4
DEPTH, CORES = 8, 2
GROUP = 8
SPAN = 32
VMEM = pl.BlockSpec(memory_space=pltpu.VMEM)
HBM = pl.BlockSpec(memory_space=pltpu.HBM)
SMALL = pltpu.CompilerParams(vmem_limit_bytes=8 * 1024 * 1024)
MEDIUM = pltpu.CompilerParams(vmem_limit_bytes=20 * 1024 * 1024)


def shifted(array, axis, by):
    count = lax.axis_size(axis)
    pairs = [(i, i + by) for i in range(count) if 0 <= i + by < count]
    return lax.ppermute(array, axis, pairs)


def along_plane(array, dx, dy):
    pairs = [
        (x * SIDE_Y + y, (x + dx) % SIDE_X * SIDE_Y + (y + dy) % SIDE_Y)
        for x in range(SIDE_X)
        for y in range(SIDE_Y)
    ]
    return lax.ppermute(array, "ctx", pairs)


def along_depth(array, target):
    pairs = []
    for z in range(DEPTH):
        for c in range(CORES):
            to_z, to_c = target(z, c)
            pairs.append((z * CORES + c, to_z % DEPTH * CORES + to_c))
    return lax.ppermute(array, "exp", pairs)


def near(array):
    return [
        along_depth(array, lambda z, c: (z, 1 - c)),
        along_depth(array, lambda z, c: (z ^ 1, c)),
        along_depth(array, lambda z, c: (z ^ 1, 1 - c)),
    ]


def far(arrays):
    return [along_depth(a, lambda z, c, k=k: (z + 2 * k, c)) for k, a in enumerate(arrays) if k]


def silu(v):
    return v / (1.0 + jnp.exp(-v))


def stage_kernel(
    inner_ref, codes_ref, gate_ref, taps_ref, bias_ref, proj_ref, rates_ref, skip_ref,
    conv_out, codes_out, gate_out, taps_out, proj_out, rates_out, skip_out,
    inner, codes, gate, bias, rates, padded, sems,
):
    moves = [
        (inner_ref, inner),
        (taps_ref, taps_out),
        (bias_ref, bias),
        (codes_ref, codes),
        (gate_ref, gate),
        (proj_ref, proj_out),
        (rates_ref, rates),
        (skip_ref, skip_out),
    ]
    copies = [pltpu.make_async_copy(a, b, sems.at[k]) for k, (a, b) in enumerate(moves)]
    for copy in copies:
        copy.start()
    length = inner.shape[0]
    count = taps_out.shape[0]
    padded[0:8, :] = jnp.zeros((8, padded.shape[1]), F32)
    for copy in copies[:3]:
        copy.wait()
    padded[8:, :] = inner[...].astype(F32)
    total = taps_out[0:1, :] * padded[8 - count + 1 : 8 - count + 1 + length, :]
    for k in range(1, count):
        start = 8 - count + 1 + k
        total = total + taps_out[k : k + 1, :] * padded[start : start + length, :]
    conv_out[...] = total + bias[...]
    for copy in copies[3:]:
        copy.wait()
    codes_out[...] = codes[...].astype(F32)
    gate_out[...] = silu(gate[...].astype(F32))
    rates_out[...] = rates[...] * (-math.log2(math.e) / 256.0)


def signal_kernel(border_ref, conv_ref, codes_ref, taps_ref, proj_ref, signal_ref, drive_ref, maps_ref):
    count = taps_ref.shape[0]
    width = conv_ref.shape[1]
    border = border_ref[...].astype(F32)
    rows = lax.broadcasted_iota(jnp.int32, (8, width), 0)
    first = jnp.zeros((8, width), F32)
    for t in range(count - 1):
        row = jnp.zeros((1, width), F32)
        for k in range(count - 1 - t):
            row = row + taps_ref[k : k + 1, :] * border[t + k : t + k + 1, :]
        first = jnp.where(rows == t, row, first)
    signal_ref[...] = silu(conv_ref[...])
    signal_ref[0:8, :] = silu(conv_ref[0:8, :] + first)
    signal = signal_ref[...]
    drive_ref[...] = jnp.minimum(codes_ref[...] * (1.0 / 256.0), 1.0) * signal
    maps_ref[...] = lax.dot_general(
        proj_ref[...],
        signal.astype(BF16),
        (((1,), (1,)), ((), ())),
        preferred_element_type=F32,
    )


def recur(maps_ref, codes_ref, drive_ref, rates, state, out_ref):
    width = codes_ref.shape[1]
    count = rates.shape[0]
    tiles = width // 128

    def group(g, state):
        rows = pl.ds(pl.multiple_of(g * SPAN, SPAN), SPAN)
        codes = codes_ref[rows, :]
        drive = drive_ref[rows, :]
        lanes = maps_ref.shape[1]
        maps = pltpu.roll(maps_ref[...], (lanes - g * SPAN) % lanes, 1)
        outs = []
        for k in range(SPAN):
            into = jnp.broadcast_to(maps[:count, k : k + 1], (count, 128))
            if out_ref is not None:
                out_of = jnp.broadcast_to(maps[count:, k : k + 1], (count, 128))
            pieces = []
            new = []
            for i in range(tiles):
                cols = slice(i * 128, (i + 1) * 128)
                decay = jnp.exp2(codes[k : k + 1, cols] * rates[:, cols])
                now = decay * state[i] + into * drive[k : k + 1, cols]
                new.append(now)
                if out_ref is not None:
                    pieces.append(jnp.sum(out_of * now, axis=0, keepdims=True))
            state = tuple(new)
            if out_ref is not None:
                outs.append(jnp.concatenate(pieces, axis=1))
        if out_ref is not None:
            out_ref[rows, :] = jnp.concatenate(outs, axis=0)
        return state

    return lax.fori_loop(0, codes_ref.shape[0] // SPAN, group, state)


def end_kernel(a_ref, b_ref, c_ref, d_ref, codes_ref, drive_ref, rates_ref, maps_ref, sent_ref):
    maps_ref[...] = (a_ref[...] + b_ref[...]) + (c_ref[...] + d_ref[...])
    rates = rates_ref[...]
    count, width = rates.shape
    zero = tuple(jnp.zeros((count, 128), F32) for _ in range(width // 128))
    state = jnp.concatenate(recur(maps_ref, codes_ref, drive_ref, rates, zero, None), axis=1)
    total = jnp.sum(codes_ref[...], axis=0, keepdims=True)
    rows = lax.broadcasted_iota(jnp.int32, (count, width), 0)
    packed = jnp.zeros((count, width), F32)
    for i in range(3):
        part = total.astype(BF16).astype(F32)
        packed = jnp.where(rows == i, part, packed)
        total = total - part
    sent_ref[...] = jnp.concatenate([state, packed], axis=0).astype(BF16)


def scan_kernel(
    ends_ref, maps_ref, codes_ref, drive_ref, signal_ref, rates_ref, skip_ref, gate_ref, proj_ref,
    own_ref, other_ref, out, arranged, gated, proj, sem,
):
    fetch = pltpu.make_async_copy(proj_ref, proj, sem)
    fetch.start()
    rates = rates_ref[...]
    count, width = rates.shape
    ctx, exp = lax.axis_index("ctx"), lax.axis_index("exp")
    x, y = ctx // SIDE_Y, ctx % SIDE_Y

    def hop(j, state):
        at = (x + SIDE_X - j // SIDE_Y) % SIDE_X * SIDE_Y + (y + SIDE_Y - j % SIDE_Y) % SIDE_Y
        block = ends_ref[pl.ds(pl.multiple_of(at * 2 * count, 2 * count), 2 * count), :].astype(F32)
        total = block[count : count + 1] + block[count + 1 : count + 2] + block[count + 2 : count + 3]
        return jnp.exp2(total * rates) * state + block[:count]

    start = lax.fori_loop(0, ctx, hop, jnp.zeros((count, width), F32))
    state = tuple(start[:, i * 128 : (i + 1) * 128] for i in range(width // 128))
    recur(maps_ref, codes_ref, drive_ref, rates, state, out)
    z, c = exp // CORES, exp % CORES
    pairs = DEPTH // 2

    def gate(j, carry):
        rows = pl.ds(pl.multiple_of(j * GROUP, GROUP), GROUP)
        to_z, to_c = j // CORES, j % CORES
        to = ((to_c + c) % 2 * 2 + (to_z + z) % 2) * pairs + (to_z // 2 + pairs - z // 2) % pairs
        value = out[rows, :] + skip_ref[...] * signal_ref[rows, :]
        arranged[pl.ds(pl.multiple_of(to * GROUP, GROUP), GROUP), :] = value * gate_ref[rows, :]
        return carry

    lax.fori_loop(0, codes_ref.shape[0] // GROUP, gate, 0)
    gated[...] = arranged[...].astype(BF16)
    fetch.wait()
    half = own_ref.shape[0]
    step = 512

    def product(k, carry):
        cols = pl.ds(pl.multiple_of(k * step, step), step)
        block = jnp.dot(gated[...], proj[:, cols], preferred_element_type=F32)
        own_ref[:, cols] = block[:half].astype(BF16)
        other_ref[:, cols] = block[half:].astype(BF16)
        return carry

    lax.fori_loop(0, proj.shape[1] // step, product, 0)


def state_space(
    inner_input, gate_input, step_codes, conv_weight, conv_bias, decay_rates, skip_gain, state_proj, out_proj
):
    length, width = inner_input.shape
    taps = conv_weight.shape[0]
    count = decay_rates.shape[0]
    model = out_proj.shape[1]
    border = shifted(inner_input[length - taps + 1 :], "ctx", 1)

    def wide(rows, kind=F32):
        return jax.ShapeDtypeStruct((rows, width), kind)

    maps_shape = jax.ShapeDtypeStruct((2 * count, length), F32)
    conv, codes, gate, taps_in, proj, rates, skip = pl.pallas_call(
        stage_kernel,
        out_shape=(
            wide(length), wide(length), wide(length), wide(taps), wide(2 * count, BF16), wide(count), wide(1),
        ),
        in_specs=[HBM] * 8,
        out_specs=(VMEM,) * 7,
        scratch_shapes=[
            pltpu.VMEM((length, width), BF16),
            pltpu.VMEM((length, width), jnp.int32),
            pltpu.VMEM((length, width), BF16),
            pltpu.VMEM((1, width), F32),
            pltpu.VMEM((count, width), F32),
            pltpu.VMEM((length + 8, width), F32),
            pltpu.SemaphoreType.DMA((8,)),
        ],
        compiler_params=SMALL,
        cost_estimate=pl.CostEstimate(flops=1 << 20, bytes_accessed=8 << 20, transcendentals=1 << 16),
        name="stage",
    )(
        *in_hbm(
            inner_input,
            step_codes,
            gate_input,
            conv_weight,
            conv_bias[None],
            state_proj.T,
            decay_rates,
            skip_gain[None],
        )
    )
    signal, drive, part = pl.pallas_call(
        signal_kernel,
        out_shape=(wide(length), wide(length), maps_shape),
        in_specs=[VMEM] * 5,
        out_specs=(VMEM,) * 3,
        compiler_params=SMALL,
        name="signal",
    )(border, conv, codes, taps_in, proj)
    part = sum(near(part), part)
    maps, sent = pl.pallas_call(
        end_kernel,
        out_shape=(maps_shape, wide(2 * count, BF16)),
        in_specs=[VMEM] * 7,
        out_specs=(VMEM,) * 2,
        compiler_params=SMALL,
        name="end_state",
    )(part, *far([part] * (DEPTH // 2)), codes, drive, rates)
    ends = join([sent] + [along_plane(sent, 0, k) for k in range(1, SIDE_Y)])
    ends = join([ends] + [along_plane(ends, k, 0) for k in range(1, SIDE_X)])
    half = jax.ShapeDtypeStruct((length // 2, model), BF16)
    return pl.pallas_call(
        scan_kernel,
        out_shape=(half, half),
        in_specs=[VMEM] * 8 + [HBM],
        out_specs=(VMEM,) * 2,
        scratch_shapes=[
            pltpu.VMEM((length, width), F32),
            pltpu.VMEM((length, width), F32),
            pltpu.VMEM((length, width), BF16),
            pltpu.VMEM((width, model), BF16),
            pltpu.SemaphoreType.DMA,
        ],
        compiler_params=MEDIUM,
        name="scan",
    )(ends, maps, codes, drive, signal, rates, skip, gate, *in_hbm(out_proj))


def join_kernel(*refs):
    out = refs[-1]
    at = 0
    for ref in refs[:-1]:
        out[at : at + ref.shape[0], :] = ref[...]
        at += ref.shape[0]


def join(arrays):
    rows = sum(a.shape[0] for a in arrays)
    return pl.pallas_call(
        join_kernel,
        out_shape=jax.ShapeDtypeStruct((rows,) + arrays[0].shape[1:], arrays[0].dtype),
        in_specs=[VMEM] * len(arrays),
        out_specs=VMEM,
        compiler_params=SMALL,
        name="join",
    )(*arrays)


def in_hbm(*arrays):
    return [pltpu.with_memory_space_constraint(a, pltpu.HBM) for a in arrays]


def added(*arrays):
    return sum(a.astype(F32) for a in arrays).astype(BF16)


def sum_out(own, other):
    pair = added(own, along_depth(other, lambda z, c: (z, 1 - c)))
    half = pair.shape[0] // 2
    chip = added(pair[:half], along_depth(pair[half:], lambda z, c: (z ^ 1, c)))
    blocks = [chip[k * GROUP : (k + 1) * GROUP] for k in range(DEPTH // 2)]
    return sum((a.astype(F32) for a in far(blocks)), blocks[0].astype(F32))


def expert_kernel(count, *refs):
    pieces, (up_ref, down_ref), outs = refs[:count], refs[count : count + 2], refs[count + 2 : 2 * count + 2]
    rows, hidden = refs[2 * count + 2 :]
    step = 256
    places = []
    at = 0
    for ref in pieces:
        places.append(slice(at, at + ref.shape[0]))
        rows[places[-1], :] = ref[...]
        at += ref.shape[0]
    for k in range(up_ref.shape[1] // step):
        cols = slice(k * step, (k + 1) * step)
        block = jnp.dot(rows[...], up_ref[:, cols], preferred_element_type=F32)
        hidden[:, cols] = silu(block).astype(BF16)

    def down(k, carry):
        cols = pl.ds(pl.multiple_of(k * step, step), step)
        block = jnp.dot(hidden[...], down_ref[:, cols], preferred_element_type=F32).astype(BF16)
        for place, out in zip(places, outs):
            out[:, cols] = block[place]
        return carry

    lax.fori_loop(0, down_ref.shape[1] // step, down, 0)


def expert(pieces, up, down):
    size = sum(p.shape[0] for p in pieces)
    model, width = up.shape
    return pl.pallas_call(
        functools.partial(expert_kernel, len(pieces)),
        out_shape=tuple(jax.ShapeDtypeStruct(p.shape, BF16) for p in pieces),
        in_specs=[VMEM] * (len(pieces) + 2),
        out_specs=(VMEM,) * len(pieces),
        scratch_shapes=[pltpu.VMEM((size, model), BF16), pltpu.VMEM((size, width), BF16)],
        compiler_params=MEDIUM,
        cost_estimate=pl.CostEstimate(
            flops=4 * size * model * width, bytes_accessed=4 * size * model, transcendentals=size * width
        ),
        name="expert",
    )(*pieces, up, down)


def fetch_kernel(after_ref, up_ref, down_ref, up_out, down_out, sems):
    up = pltpu.make_async_copy(up_ref, up_out, sems.at[0])
    down = pltpu.make_async_copy(down_ref, down_out, sems.at[1])
    up.start()
    down.start()
    up.wait()
    down.wait()


def fetch(after, up, down):
    return pl.pallas_call(
        fetch_kernel,
        out_shape=(jax.ShapeDtypeStruct(up.shape, BF16), jax.ShapeDtypeStruct(down.shape, BF16)),
        in_specs=[pl.BlockSpec(memory_space=pl.ANY), HBM, HBM],
        out_specs=(VMEM, VMEM),
        scratch_shapes=[pltpu.SemaphoreType.DMA((2,))],
        compiler_params=SMALL,
        cost_estimate=pl.CostEstimate(flops=0, bytes_accessed=32 << 20, transcendentals=0),
        name="fetch",
    )(after, *in_hbm(up, down))


def split(array, parts):
    size = array.shape[0] // parts
    return [array[k * size : (k + 1) * size] for k in range(parts)]


def run_expert(arrived, up, down):
    sides = ((1, 0), (0, 1))
    steps = (1, 2, 3)
    gathered = []
    for (dx, dy), rows in zip(sides, split(arrived, 2)):
        gathered.append(join([rows] + [along_plane(rows, k * dx, k * dy) for k in steps]))
    after, before = [], []
    for (dy, dx), rows in zip(sides, gathered):
        after.append(along_plane(rows, dx, dy))
        before.append(along_plane(rows, -dx, -dy))
    up, down = fetch(gathered[1], up, down)
    own = expert(gathered, up, down)
    after, before, up, down, own = lax.optimization_barrier((after, before, up, down, own))
    opposite = []
    for (dy, dx), a, b in zip(sides, after, before):
        half = a.shape[0] // 2
        opposite += [along_plane(a[:half], dx, dy), along_plane(b[half:], -dx, -dy)]
    close = expert(after + before, up, down)
    remote = expert(opposite, up, down)
    passed = []
    for i, (dy, dx) in enumerate(sides):
        first, second = remote[2 * i : 2 * i + 2]
        passed += [along_plane(first, -dx, -dy), along_plane(second, dx, dy)]
    passed = lax.optimization_barrier(passed)
    sums = []
    for i, (dy, dx) in enumerate(sides):
        to_after, to_before = close[i], close[2 + i]
        half = to_after.shape[0] // 2
        one = jnp.concatenate([added(to_after[:half], passed[2 * i]), to_after[half:]])
        three = jnp.concatenate([to_before[:half], added(to_before[half:], passed[2 * i + 1])])
        sums.append(added(own[i], along_plane(one, -dx, -dy), along_plane(three, dx, dy)))
    result = []
    for (dx, dy), total in zip(sides, sums):
        blocks = split(total, 4)
        result.append(added(blocks[0], *[along_plane(blocks[k], -k * dx, -k * dy) for k in steps]))
    return jnp.concatenate(result)


def shards(
    inner_input,
    gate_input,
    step_codes,
    conv_weight,
    conv_bias,
    decay_rates,
    skip_gain,
    state_proj,
    out_proj,
    residual,
    norm_gain,
    expert_ids,
    gate_codes,
    up_weight,
    down_weight,
):
    own, other = state_space(
        inner_input,
        gate_input,
        step_codes,
        conv_weight,
        conv_bias,
        decay_rates,
        skip_gain,
        state_proj,
        out_proj,
    )
    row_count = residual.shape[0]
    mamba_out = sum_out(own, other)
    stream = (residual.astype(F32) + mamba_out).astype(BF16)
    stream_wide = stream.astype(F32)
    normed = (
        stream_wide
        * lax.rsqrt(jnp.mean(stream_wide * stream_wide, axis=-1, keepdims=True) + 1e-05)
        * norm_gain
    ).astype(BF16)
    experts = lax.axis_size("exp") * up_weight.shape[0]
    top_count = expert_ids.shape[1]
    capacity = max(2, 4 * row_count // experts)
    onehot = (
        (expert_ids[:, :, None] == jnp.arange(experts)[None, None, :])
        .astype(jnp.int32)
        .reshape(row_count * top_count, experts)
    )
    before = jnp.cumsum(onehot, axis=0) - onehot
    ranking = jnp.sum(before * onehot, axis=1).reshape(row_count, top_count)
    slot_index = expert_ids * capacity + ranking
    slots = slot_index[:, :, None] == jnp.arange(experts * capacity)[None, None, :]
    dispatch_table = jnp.any(slots, axis=1).astype(BF16)
    up_local = up_weight[0]
    down_local = down_weight[0]
    outgoing = lax.dot_general(
        dispatch_table, normed, (((0,), (0,)), ((), ())), preferred_element_type=F32
    ).astype(BF16)
    arrived = lax.all_to_all(outgoing, "exp", split_axis=0, concat_axis=0, tiled=True)
    expert_out = run_expert(arrived, up_local, down_local)
    returned = lax.all_to_all(expert_out, "exp", split_axis=0, concat_axis=0, tiled=True)
    gate_weights = gate_codes.astype(F32)
    gate_weights = gate_weights / jnp.sum(gate_weights, axis=1, keepdims=True)
    picked = jnp.take(returned, slot_index, axis=0).astype(F32)
    mixture_out = jnp.sum(gate_weights[:, :, None] * picked, axis=1)
    return (stream_wide + mixture_out).astype(BF16)


def solution(mesh):
    return jax.shard_map(
        shards,
        mesh=mesh,
        in_specs=(
            P("ctx", "exp"),
            P("ctx", "exp"),
            P("ctx", "exp"),
            P(None, "exp"),
            P("exp"),
            P(None, "exp"),
            P("exp"),
            P("exp", None),
            P("exp", None),
            P(("ctx", "exp"), None),
            P(),
            P(("ctx", "exp"), None),
            P(("ctx", "exp"), None),
            P("exp", None, "ctx"),
            P("exp", "ctx", None),
        ),
        out_specs=P(("ctx", "exp"), None),
        check_vma=False,
    )
```

```python
import functools
import math
import jax
import jax.numpy as jnp
from jax import lax
from jax.experimental import pallas as pl
from jax.experimental.pallas import tpu as pltpu
from jax.sharding import PartitionSpec as P

F32 = jnp.float32
BF16 = jnp.bfloat16
SIDE_X, SIDE_Y = 4, 4
DEPTH, CORES = 8, 2
GROUP = 8
SPAN = 32
VMEM = pl.BlockSpec(memory_space=pltpu.VMEM)
HBM = pl.BlockSpec(memory_space=pltpu.HBM)
SMALL = pltpu.CompilerParams(vmem_limit_bytes=8 * 1024 * 1024)
MEDIUM = pltpu.CompilerParams(vmem_limit_bytes=20 * 1024 * 1024)


def shifted(array, axis, by):
    count = lax.axis_size(axis)
    pairs = [(i, i + by) for i in range(count) if 0 <= i + by < count]
    return lax.ppermute(array, axis, pairs)


def along_plane(array, dx, dy):
    pairs = [
        (x * SIDE_Y + y, (x + dx) % SIDE_X * SIDE_Y + (y + dy) % SIDE_Y)
        for x in range(SIDE_X)
        for y in range(SIDE_Y)
    ]
    return lax.ppermute(array, "ctx", pairs)


def along_depth(array, target):
    pairs = []
    for z in range(DEPTH):
        for c in range(CORES):
            to_z, to_c = target(z, c)
            pairs.append((z * CORES + c, to_z % DEPTH * CORES + to_c))
    return lax.ppermute(array, "exp", pairs)


def near(array):
    return [
        along_depth(array, lambda z, c: (z, 1 - c)),
        along_depth(array, lambda z, c: (z ^ 1, c)),
        along_depth(array, lambda z, c: (z ^ 1, 1 - c)),
    ]


def far(arrays):
    return [along_depth(a, lambda z, c, k=k: (z + 2 * k, c)) for k, a in enumerate(arrays) if k]


def silu(v):
    return v / (1.0 + jnp.exp(-v))


def stage_kernel(
    inner_ref, codes_ref, gate_ref, taps_ref, bias_ref, proj_ref, rates_ref, skip_ref,
    conv_out, codes_out, gate_out, taps_out, proj_out, rates_out, skip_out,
    inner, codes, gate, bias, rates, padded, sems,
):
    moves = [
        (inner_ref, inner),
        (taps_ref, taps_out),
        (bias_ref, bias),
        (codes_ref, codes),
        (gate_ref, gate),
        (proj_ref, proj_out),
        (rates_ref, rates),
        (skip_ref, skip_out),
    ]
    copies = [pltpu.make_async_copy(a, b, sems.at[k]) for k, (a, b) in enumerate(moves)]
    for copy in copies:
        copy.start()
    length = inner.shape[0]
    count = taps_out.shape[0]
    padded[0:8, :] = jnp.zeros((8, padded.shape[1]), F32)
    for copy in copies[:3]:
        copy.wait()
    padded[8:, :] = inner[...].astype(F32)
    total = taps_out[0:1, :] * padded[8 - count + 1 : 8 - count + 1 + length, :]
    for k in range(1, count):
        start = 8 - count + 1 + k
        total = total + taps_out[k : k + 1, :] * padded[start : start + length, :]
    conv_out[...] = total + bias[...]
    for copy in copies[3:]:
        copy.wait()
    codes_out[...] = codes[...].astype(F32)
    gate_out[...] = silu(gate[...].astype(F32))
    rates_out[...] = rates[...] * (-math.log2(math.e) / 256.0)


def signal_kernel(border_ref, conv_ref, codes_ref, taps_ref, proj_ref, signal_ref, drive_ref, maps_ref):
    count = taps_ref.shape[0]
    width = conv_ref.shape[1]
    border = border_ref[...].astype(F32)
    rows = lax.broadcasted_iota(jnp.int32, (8, width), 0)
    first = jnp.zeros((8, width), F32)
    for t in range(count - 1):
        row = jnp.zeros((1, width), F32)
        for k in range(count - 1 - t):
            row = row + taps_ref[k : k + 1, :] * border[t + k : t + k + 1, :]
        first = jnp.where(rows == t, row, first)
    signal_ref[...] = silu(conv_ref[...])
    signal_ref[0:8, :] = silu(conv_ref[0:8, :] + first)
    signal = signal_ref[...]
    drive_ref[...] = jnp.minimum(codes_ref[...] * (1.0 / 256.0), 1.0) * signal
    maps_ref[...] = lax.dot_general(
        proj_ref[...],
        signal.astype(BF16),
        (((1,), (1,)), ((), ())),
        preferred_element_type=F32,
    )


def recur(maps_ref, codes_ref, drive_ref, rates, state, out_ref):
    width = codes_ref.shape[1]
    count = rates.shape[0]
    tiles = width // 128

    def group(g, state):
        rows = pl.ds(pl.multiple_of(g * SPAN, SPAN), SPAN)
        codes = codes_ref[rows, :]
        drive = drive_ref[rows, :]
        lanes = maps_ref.shape[1]
        maps = pltpu.roll(maps_ref[...], (lanes - g * SPAN) % lanes, 1)
        outs = []
        for k in range(SPAN):
            into = jnp.broadcast_to(maps[:count, k : k + 1], (count, 128))
            if out_ref is not None:
                out_of = jnp.broadcast_to(maps[count:, k : k + 1], (count, 128))
            pieces = []
            new = []
            for i in range(tiles):
                cols = slice(i * 128, (i + 1) * 128)
                decay = jnp.exp2(codes[k : k + 1, cols] * rates[:, cols])
                now = decay * state[i] + into * drive[k : k + 1, cols]
                new.append(now)
                if out_ref is not None:
                    pieces.append(jnp.sum(out_of * now, axis=0, keepdims=True))
            state = tuple(new)
            if out_ref is not None:
                outs.append(jnp.concatenate(pieces, axis=1))
        if out_ref is not None:
            out_ref[rows, :] = jnp.concatenate(outs, axis=0)
        return state

    return lax.fori_loop(0, codes_ref.shape[0] // SPAN, group, state)


def end_kernel(a_ref, b_ref, c_ref, d_ref, codes_ref, drive_ref, rates_ref, maps_ref, sent_ref):
    maps_ref[...] = (a_ref[...] + b_ref[...]) + (c_ref[...] + d_ref[...])
    rates = rates_ref[...]
    count, width = rates.shape
    zero = tuple(jnp.zeros((count, 128), F32) for _ in range(width // 128))
    state = jnp.concatenate(recur(maps_ref, codes_ref, drive_ref, rates, zero, None), axis=1)
    sent_ref[...] = packed(state, jnp.sum(codes_ref[...], axis=0, keepdims=True))


def packed(state, total):
    rows = lax.broadcasted_iota(jnp.int32, state.shape, 0)
    parts = jnp.zeros(state.shape, F32)
    for i in range(3):
        part = total.astype(BF16).astype(F32)
        parts = jnp.where(rows == i, part, parts)
        total = total - part
    return jnp.concatenate([state, parts], axis=0).astype(BF16)


def unpacked(ref, k, count):
    block = ref[pl.ds(pl.multiple_of(k * 2 * count, 2 * count), 2 * count), :].astype(F32)
    return block[:count], block[count : count + 1] + block[count + 1 : count + 2] + block[count + 2 : count + 3]


def follow(ref, k, rates, state):
    end, total = unpacked(ref, k, rates.shape[0])
    return jnp.exp2(total * rates) * state + end


def line_kernel(a_ref, b_ref, c_ref, d_ref, rates_ref, ends_ref, sent_ref):
    rates = rates_ref[...]
    count, width = rates.shape
    for k, ref in enumerate((a_ref, b_ref, c_ref, d_ref)):
        ends_ref[2 * count * k : 2 * count * (k + 1), :] = ref[...]
    y = lax.axis_index("ctx") % SIDE_Y

    def one(j, carry):
        state, total = carry
        at = (y + SIDE_Y - j) % SIDE_Y
        end, more = unpacked(ends_ref, at, count)
        return jnp.exp2(more * rates) * state + end, total + more

    state, total = lax.fori_loop(
        0, SIDE_Y, one, (jnp.zeros((count, width), F32), jnp.zeros((1, width), F32))
    )
    sent_ref[...] = packed(state, total)


def scan_kernel(
    rows_ref, ends_ref, maps_ref, codes_ref, drive_ref, signal_ref, rates_ref, skip_ref, gate_ref, proj_ref,
    own_ref, other_ref, out, arranged, gated, proj, sem,
):
    fetch = pltpu.make_async_copy(proj_ref, proj, sem)
    fetch.start()
    rates = rates_ref[...]
    count, width = rates.shape
    ctx, exp = lax.axis_index("ctx"), lax.axis_index("exp")
    x, y = ctx // SIDE_Y, ctx % SIDE_Y

    zero = jnp.zeros((count, width), F32)
    start = lax.fori_loop(0, x, lambda j, state: follow(rows_ref, (x - j), rates, state), zero)
    start = lax.fori_loop(0, y, lambda j, state: follow(ends_ref, (y - j), rates, state), start)
    state = tuple(start[:, i * 128 : (i + 1) * 128] for i in range(width // 128))
    recur(maps_ref, codes_ref, drive_ref, rates, state, out)
    z, c = exp // CORES, exp % CORES

    def gate(j, carry):
        rows = pl.ds(pl.multiple_of(j * GROUP, GROUP), GROUP)
        away = (j // CORES + DEPTH - z) % DEPTH
        to = (j % CORES + c) % CORES * DEPTH + away % 2 * (DEPTH // 2) + away // 2
        value = out[rows, :] + skip_ref[...] * signal_ref[rows, :]
        arranged[pl.ds(pl.multiple_of(to * GROUP, GROUP), GROUP), :] = value * gate_ref[rows, :]
        return carry

    lax.fori_loop(0, codes_ref.shape[0] // GROUP, gate, 0)
    gated[...] = arranged[...].astype(BF16)
    fetch.wait()
    half = own_ref.shape[0]
    step = 512

    def product(k, carry):
        cols = pl.ds(pl.multiple_of(k * step, step), step)
        block = jnp.dot(gated[...], proj[:, cols], preferred_element_type=F32)
        own_ref[:, cols] = block[:half].astype(BF16)
        other_ref[:, cols] = block[half:].astype(BF16)
        return carry

    lax.fori_loop(0, proj.shape[1] // step, product, 0)


def state_space(
    inner_input, gate_input, step_codes, conv_weight, conv_bias, decay_rates, skip_gain, state_proj, out_proj
):
    length, width = inner_input.shape
    taps = conv_weight.shape[0]
    count = decay_rates.shape[0]
    model = out_proj.shape[1]
    border = shifted(inner_input[length - taps + 1 :], "ctx", 1)

    def wide(rows, kind=F32):
        return jax.ShapeDtypeStruct((rows, width), kind)

    maps_shape = jax.ShapeDtypeStruct((2 * count, length), F32)
    conv, codes, gate, taps_in, proj, rates, skip = pl.pallas_call(
        stage_kernel,
        out_shape=(
            wide(length), wide(length), wide(length), wide(taps), wide(2 * count, BF16), wide(count), wide(1),
        ),
        in_specs=[HBM] * 8,
        out_specs=(VMEM,) * 7,
        scratch_shapes=[
            pltpu.VMEM((length, width), BF16),
            pltpu.VMEM((length, width), jnp.int32),
            pltpu.VMEM((length, width), BF16),
            pltpu.VMEM((1, width), F32),
            pltpu.VMEM((count, width), F32),
            pltpu.VMEM((length + 8, width), F32),
            pltpu.SemaphoreType.DMA((8,)),
        ],
        compiler_params=SMALL,
        cost_estimate=pl.CostEstimate(flops=1 << 20, bytes_accessed=8 << 20, transcendentals=1 << 16),
        name="stage",
    )(
        *in_hbm(
            inner_input,
            step_codes,
            gate_input,
            conv_weight,
            conv_bias[None],
            state_proj.T,
            decay_rates,
            skip_gain[None],
        )
    )
    signal, drive, part = pl.pallas_call(
        signal_kernel,
        out_shape=(wide(length), wide(length), maps_shape),
        in_specs=[VMEM] * 5,
        out_specs=(VMEM,) * 3,
        compiler_params=SMALL,
        name="signal",
    )(border, conv, codes, taps_in, proj)
    part = sum(near(part), part)
    maps, sent = pl.pallas_call(
        end_kernel,
        out_shape=(maps_shape, wide(2 * count, BF16)),
        in_specs=[VMEM] * 7,
        out_specs=(VMEM,) * 2,
        compiler_params=SMALL,
        name="end_state",
    )(part, *far([part] * (DEPTH // 2)), codes, drive, rates)
    ends, line = pl.pallas_call(
        line_kernel,
        out_shape=(wide(2 * count * SIDE_Y, BF16), wide(2 * count, BF16)),
        in_specs=[VMEM] * 5,
        out_specs=(VMEM,) * 2,
        compiler_params=SMALL,
        name="line",
    )(sent, *[along_plane(sent, 0, k) for k in range(1, SIDE_Y)], rates)
    rows = join([line] + [along_plane(line, k, 0) for k in range(1, SIDE_X)])
    half = jax.ShapeDtypeStruct((length // 2, model), BF16)
    return pl.pallas_call(
        scan_kernel,
        out_shape=(half, half),
        in_specs=[VMEM] * 9 + [HBM],
        out_specs=(VMEM,) * 2,
        scratch_shapes=[
            pltpu.VMEM((length, width), F32),
            pltpu.VMEM((length, width), F32),
            pltpu.VMEM((length, width), BF16),
            pltpu.VMEM((width, model), BF16),
            pltpu.SemaphoreType.DMA,
        ],
        compiler_params=MEDIUM,
        name="scan",
    )(rows, ends, maps, codes, drive, signal, rates, skip, gate, *in_hbm(out_proj))


def join_kernel(*refs):
    out = refs[-1]
    at = 0
    for ref in refs[:-1]:
        out[at : at + ref.shape[0], :] = ref[...]
        at += ref.shape[0]


def join(arrays):
    rows = sum(a.shape[0] for a in arrays)
    return pl.pallas_call(
        join_kernel,
        out_shape=jax.ShapeDtypeStruct((rows,) + arrays[0].shape[1:], arrays[0].dtype),
        in_specs=[VMEM] * len(arrays),
        out_specs=VMEM,
        compiler_params=SMALL,
        name="join",
    )(*arrays)


def in_hbm(*arrays):
    return [pltpu.with_memory_space_constraint(a, pltpu.HBM) for a in arrays]


def added(*arrays):
    return sum(a.astype(F32) for a in arrays).astype(BF16)


def sum_out(own, other):
    pair = added(own, along_depth(other, lambda z, c: (z, 1 - c)))
    even, up, down = pair[: 4 * GROUP], pair[4 * GROUP : 6 * GROUP], pair[6 * GROUP :]
    low = split(along_depth(up, lambda z, c: (z + 1, c)), 2)
    high = split(along_depth(down, lambda z, c: (z - 1, c)), 2)
    even = split(even, 4)
    blocks = [added(even[0], low[0], high[1]), added(even[1], low[1]), even[2], added(even[3], high[0])]
    return sum((a.astype(F32) for a in far(blocks)), blocks[0].astype(F32))


def expert_kernel(count, *refs):
    pieces, (up_ref, down_ref), outs = refs[:count], refs[count : count + 2], refs[count + 2 : 2 * count + 2]
    rows, hidden = refs[2 * count + 2 :]
    step = 256
    places = []
    at = 0
    for ref in pieces:
        places.append(slice(at, at + ref.shape[0]))
        rows[places[-1], :] = ref[...]
        at += ref.shape[0]
    for k in range(up_ref.shape[1] // step):
        cols = slice(k * step, (k + 1) * step)
        block = jnp.dot(rows[...], up_ref[:, cols], preferred_element_type=F32)
        hidden[:, cols] = silu(block).astype(BF16)

    def down(k, carry):
        cols = pl.ds(pl.multiple_of(k * step, step), step)
        block = jnp.dot(hidden[...], down_ref[:, cols], preferred_element_type=F32).astype(BF16)
        for place, out in zip(places, outs):
            out[:, cols] = block[place]
        return carry

    lax.fori_loop(0, down_ref.shape[1] // step, down, 0)


def expert(pieces, up, down):
    size = sum(p.shape[0] for p in pieces)
    model, width = up.shape
    return pl.pallas_call(
        functools.partial(expert_kernel, len(pieces)),
        out_shape=tuple(jax.ShapeDtypeStruct(p.shape, BF16) for p in pieces),
        in_specs=[VMEM] * (len(pieces) + 2),
        out_specs=(VMEM,) * len(pieces),
        scratch_shapes=[pltpu.VMEM((size, model), BF16), pltpu.VMEM((size, width), BF16)],
        compiler_params=MEDIUM,
        cost_estimate=pl.CostEstimate(
            flops=4 * size * model * width, bytes_accessed=4 * size * model, transcendentals=size * width
        ),
        name="expert",
    )(*pieces, up, down)


def fetch_kernel(after_ref, up_ref, down_ref, up_out, down_out, sems):
    up = pltpu.make_async_copy(up_ref, up_out, sems.at[0])
    down = pltpu.make_async_copy(down_ref, down_out, sems.at[1])
    up.start()
    down.start()
    up.wait()
    down.wait()


def fetch(after, up, down):
    return pl.pallas_call(
        fetch_kernel,
        out_shape=(jax.ShapeDtypeStruct(up.shape, BF16), jax.ShapeDtypeStruct(down.shape, BF16)),
        in_specs=[pl.BlockSpec(memory_space=pl.ANY), HBM, HBM],
        out_specs=(VMEM, VMEM),
        scratch_shapes=[pltpu.SemaphoreType.DMA((2,))],
        compiler_params=SMALL,
        cost_estimate=pl.CostEstimate(flops=0, bytes_accessed=32 << 20, transcendentals=0),
        name="fetch",
    )(after, *in_hbm(up, down))


def split(array, parts):
    size = array.shape[0] // parts
    return [array[k * size : (k + 1) * size] for k in range(parts)]


def run_expert(arrived, up, down):
    sides = ((1, 0), (0, 1))
    steps = (1, 2, 3)
    gathered = []
    for (dx, dy), rows in zip(sides, split(arrived, 2)):
        gathered.append(join([rows] + [along_plane(rows, k * dx, k * dy) for k in steps]))
    after, before = [], []
    for (dy, dx), rows in zip(sides, gathered):
        after.append(along_plane(rows, dx, dy))
        before.append(along_plane(rows, -dx, -dy))
    up, down = fetch(gathered[1], up, down)
    own = expert(gathered, up, down)
    after, before, up, down, own = lax.optimization_barrier((after, before, up, down, own))
    opposite = []
    for (dy, dx), a, b in zip(sides, after, before):
        half = a.shape[0] // 2
        opposite += [along_plane(a[:half], dx, dy), along_plane(b[half:], -dx, -dy)]
    close = expert(after + before, up, down)
    remote = expert(opposite, up, down)
    passed = []
    for i, (dy, dx) in enumerate(sides):
        first, second = remote[2 * i : 2 * i + 2]
        passed += [along_plane(first, -dx, -dy), along_plane(second, dx, dy)]
    passed = lax.optimization_barrier(passed)
    sums = []
    for i, (dy, dx) in enumerate(sides):
        to_after, to_before = close[i], close[2 + i]
        half = to_after.shape[0] // 2
        one = jnp.concatenate([added(to_after[:half], passed[2 * i]), to_after[half:]])
        three = jnp.concatenate([to_before[:half], added(to_before[half:], passed[2 * i + 1])])
        sums.append(added(own[i], along_plane(one, -dx, -dy), along_plane(three, dx, dy)))
    result = []
    for (dx, dy), total in zip(sides, sums):
        blocks = split(total, 4)
        result.append(added(blocks[0], *[along_plane(blocks[k], -k * dx, -k * dy) for k in steps]))
    return jnp.concatenate(result)


def shards(
    inner_input,
    gate_input,
    step_codes,
    conv_weight,
    conv_bias,
    decay_rates,
    skip_gain,
    state_proj,
    out_proj,
    residual,
    norm_gain,
    expert_ids,
    gate_codes,
    up_weight,
    down_weight,
):
    own, other = state_space(
        inner_input,
        gate_input,
        step_codes,
        conv_weight,
        conv_bias,
        decay_rates,
        skip_gain,
        state_proj,
        out_proj,
    )
    row_count = residual.shape[0]
    mamba_out = sum_out(own, other)
    stream = (residual.astype(F32) + mamba_out).astype(BF16)
    stream_wide = stream.astype(F32)
    normed = (
        stream_wide
        * lax.rsqrt(jnp.mean(stream_wide * stream_wide, axis=-1, keepdims=True) + 1e-05)
        * norm_gain
    ).astype(BF16)
    experts = lax.axis_size("exp") * up_weight.shape[0]
    top_count = expert_ids.shape[1]
    capacity = max(2, 4 * row_count // experts)
    onehot = (
        (expert_ids[:, :, None] == jnp.arange(experts)[None, None, :])
        .astype(jnp.int32)
        .reshape(row_count * top_count, experts)
    )
    before = jnp.cumsum(onehot, axis=0) - onehot
    ranking = jnp.sum(before * onehot, axis=1).reshape(row_count, top_count)
    slot_index = expert_ids * capacity + ranking
    slots = slot_index[:, :, None] == jnp.arange(experts * capacity)[None, None, :]
    dispatch_table = jnp.any(slots, axis=1).astype(BF16)
    up_local = up_weight[0]
    down_local = down_weight[0]
    outgoing = lax.dot_general(
        dispatch_table, normed, (((0,), (0,)), ((), ())), preferred_element_type=F32
    ).astype(BF16)
    arrived = lax.all_to_all(outgoing, "exp", split_axis=0, concat_axis=0, tiled=True)
    expert_out = run_expert(arrived, up_local, down_local)
    returned = lax.all_to_all(expert_out, "exp", split_axis=0, concat_axis=0, tiled=True)
    gate_weights = gate_codes.astype(F32)
    gate_weights = gate_weights / jnp.sum(gate_weights, axis=1, keepdims=True)
    table = jnp.sum(gate_weights[:, :, None] * slots.astype(F32), axis=1)
    mixture_out = jnp.dot(table, returned.astype(F32), precision=lax.Precision.HIGHEST)
    return (stream_wide + mixture_out).astype(BF16)


def solution(mesh):
    return jax.shard_map(
        shards,
        mesh=mesh,
        in_specs=(
            P("ctx", "exp"),
            P("ctx", "exp"),
            P("ctx", "exp"),
            P(None, "exp"),
            P("exp"),
            P(None, "exp"),
            P("exp"),
            P("exp", None),
            P("exp", None),
            P(("ctx", "exp"), None),
            P(),
            P(("ctx", "exp"), None),
            P(("ctx", "exp"), None),
            P("exp", None, "ctx"),
            P("exp", "ctx", None),
        ),
        out_specs=P(("ctx", "exp"), None),
        check_vma=False,
    )
```

```python
import functools
import math
import jax
import jax.numpy as jnp
from jax import lax
from jax.experimental import pallas as pl
from jax.experimental.pallas import tpu as pltpu
from jax.sharding import PartitionSpec as P

F32 = jnp.float32
BF16 = jnp.bfloat16
SIDE_X, SIDE_Y = 4, 4
DEPTH, CORES = 8, 2
GROUP = 8
SPAN = 32
VMEM = pl.BlockSpec(memory_space=pltpu.VMEM)
HBM = pl.BlockSpec(memory_space=pltpu.HBM)
SMALL = pltpu.CompilerParams(vmem_limit_bytes=8 * 1024 * 1024)
MEDIUM = pltpu.CompilerParams(vmem_limit_bytes=20 * 1024 * 1024)


def shifted(array, axis, by):
    count = lax.axis_size(axis)
    pairs = [(i, i + by) for i in range(count) if 0 <= i + by < count]
    return lax.ppermute(array, axis, pairs)


def along_plane(array, dx, dy):
    pairs = [
        (x * SIDE_Y + y, (x + dx) % SIDE_X * SIDE_Y + (y + dy) % SIDE_Y)
        for x in range(SIDE_X)
        for y in range(SIDE_Y)
    ]
    return lax.ppermute(array, "ctx", pairs)


def along_depth(array, target):
    pairs = []
    for z in range(DEPTH):
        for c in range(CORES):
            to_z, to_c = target(z, c)
            pairs.append((z * CORES + c, to_z % DEPTH * CORES + to_c))
    return lax.ppermute(array, "exp", pairs)


def near(array):
    return [
        along_depth(array, lambda z, c: (z, 1 - c)),
        along_depth(array, lambda z, c: (z ^ 1, c)),
        along_depth(array, lambda z, c: (z ^ 1, 1 - c)),
    ]


def far(arrays):
    return [along_depth(a, lambda z, c, k=k: (z + 2 * k, c)) for k, a in enumerate(arrays) if k]


def silu(v):
    return v / (1.0 + jnp.exp(-v))


def stage_kernel(
    inner_ref, codes_ref, gate_ref, taps_ref, bias_ref, proj_ref, rates_ref, skip_ref,
    conv_out, codes_out, gate_out, taps_out, proj_out, rates_out, skip_out,
    inner, codes, gate, bias, rates, padded, sems,
):
    moves = [
        (inner_ref, inner),
        (taps_ref, taps_out),
        (bias_ref, bias),
        (codes_ref, codes),
        (gate_ref, gate),
        (proj_ref, proj_out),
        (rates_ref, rates),
        (skip_ref, skip_out),
    ]
    copies = [pltpu.make_async_copy(a, b, sems.at[k]) for k, (a, b) in enumerate(moves)]
    for copy in copies:
        copy.start()
    length = inner.shape[0]
    count = taps_out.shape[0]
    padded[0:8, :] = jnp.zeros((8, padded.shape[1]), F32)
    for copy in copies[:3]:
        copy.wait()
    padded[8:, :] = inner[...].astype(F32)
    total = taps_out[0:1, :] * padded[8 - count + 1 : 8 - count + 1 + length, :]
    for k in range(1, count):
        start = 8 - count + 1 + k
        total = total + taps_out[k : k + 1, :] * padded[start : start + length, :]
    conv_out[...] = total + bias[...]
    for copy in copies[3:]:
        copy.wait()
    codes_out[...] = codes[...].astype(F32)
    gate_out[...] = silu(gate[...].astype(F32))
    rates_out[...] = rates[...] * (-math.log2(math.e) / 256.0)


def signal_kernel(border_ref, conv_ref, codes_ref, taps_ref, proj_ref, signal_ref, drive_ref, maps_ref):
    count = taps_ref.shape[0]
    width = conv_ref.shape[1]
    border = border_ref[...].astype(F32)
    rows = lax.broadcasted_iota(jnp.int32, (8, width), 0)
    first = jnp.zeros((8, width), F32)
    for t in range(count - 1):
        row = jnp.zeros((1, width), F32)
        for k in range(count - 1 - t):
            row = row + taps_ref[k : k + 1, :] * border[t + k : t + k + 1, :]
        first = jnp.where(rows == t, row, first)
    signal_ref[...] = silu(conv_ref[...])
    signal_ref[0:8, :] = silu(conv_ref[0:8, :] + first)
    signal = signal_ref[...]
    drive_ref[...] = jnp.minimum(codes_ref[...] * (1.0 / 256.0), 1.0) * signal
    maps_ref[...] = lax.dot_general(
        proj_ref[...],
        signal.astype(BF16),
        (((1,), (1,)), ((), ())),
        preferred_element_type=F32,
    )


def recur(maps_ref, codes_ref, drive_ref, rates, state, out_ref):
    width = codes_ref.shape[1]
    count = rates.shape[0]
    tiles = width // 128

    def group(g, state):
        rows = pl.ds(pl.multiple_of(g * SPAN, SPAN), SPAN)
        codes = codes_ref[rows, :]
        drive = drive_ref[rows, :]
        lanes = maps_ref.shape[1]
        maps = pltpu.roll(maps_ref[...], (lanes - g * SPAN) % lanes, 1)
        outs = []
        for k in range(SPAN):
            into = jnp.broadcast_to(maps[:count, k : k + 1], (count, 128))
            if out_ref is not None:
                out_of = jnp.broadcast_to(maps[count:, k : k + 1], (count, 128))
            pieces = []
            new = []
            for i in range(tiles):
                cols = slice(i * 128, (i + 1) * 128)
                decay = jnp.exp2(codes[k : k + 1, cols] * rates[:, cols])
                now = decay * state[i] + into * drive[k : k + 1, cols]
                new.append(now)
                if out_ref is not None:
                    pieces.append(jnp.sum(out_of * now, axis=0, keepdims=True))
            state = tuple(new)
            if out_ref is not None:
                outs.append(jnp.concatenate(pieces, axis=1))
        if out_ref is not None:
            out_ref[rows, :] = jnp.concatenate(outs, axis=0)
        return state

    return lax.fori_loop(0, codes_ref.shape[0] // SPAN, group, state)


def end_kernel(a_ref, b_ref, c_ref, d_ref, codes_ref, drive_ref, rates_ref, maps_ref, sent_ref):
    maps_ref[...] = (a_ref[...] + b_ref[...]) + (c_ref[...] + d_ref[...])
    rates = rates_ref[...]
    count, width = rates.shape
    zero = tuple(jnp.zeros((count, 128), F32) for _ in range(width // 128))
    state = jnp.concatenate(recur(maps_ref, codes_ref, drive_ref, rates, zero, None), axis=1)
    sent_ref[...] = packed(state, jnp.sum(codes_ref[...], axis=0, keepdims=True))


def packed(state, total):
    rows = lax.broadcasted_iota(jnp.int32, state.shape, 0)
    parts = jnp.zeros(state.shape, F32)
    for i in range(3):
        part = total.astype(BF16).astype(F32)
        parts = jnp.where(rows == i, part, parts)
        total = total - part
    return jnp.concatenate([state, parts], axis=0).astype(BF16)


def unpacked(ref, k, count):
    block = ref[pl.ds(pl.multiple_of(k * 2 * count, 2 * count), 2 * count), :].astype(F32)
    return block[:count], block[count : count + 1] + block[count + 1 : count + 2] + block[count + 2 : count + 3]


def follow(ref, k, rates, state):
    end, total = unpacked(ref, k, rates.shape[0])
    return jnp.exp2(total * rates) * state + end


def line_kernel(a_ref, b_ref, c_ref, d_ref, rates_ref, ends_ref, sent_ref):
    rates = rates_ref[...]
    count, width = rates.shape
    for k, ref in enumerate((a_ref, b_ref, c_ref, d_ref)):
        ends_ref[2 * count * k : 2 * count * (k + 1), :] = ref[...]
    y = lax.axis_index("ctx") % SIDE_Y

    def one(j, carry):
        state, total = carry
        at = (y + SIDE_Y - j) % SIDE_Y
        end, more = unpacked(ends_ref, at, count)
        return jnp.exp2(more * rates) * state + end, total + more

    state, total = lax.fori_loop(
        0, SIDE_Y, one, (jnp.zeros((count, width), F32), jnp.zeros((1, width), F32))
    )
    sent_ref[...] = packed(state, total)


def scan_kernel(
    rows_ref, ends_ref, maps_ref, codes_ref, drive_ref, signal_ref, rates_ref, skip_ref, gate_ref, proj_ref,
    own_ref, other_ref, out, arranged, gated, proj, sem,
):
    fetch = pltpu.make_async_copy(proj_ref, proj, sem)
    fetch.start()
    rates = rates_ref[...]
    count, width = rates.shape
    ctx, exp = lax.axis_index("ctx"), lax.axis_index("exp")
    x, y = ctx // SIDE_Y, ctx % SIDE_Y

    zero = jnp.zeros((count, width), F32)
    start = lax.fori_loop(0, x, lambda j, state: follow(rows_ref, (x - j), rates, state), zero)
    start = lax.fori_loop(0, y, lambda j, state: follow(ends_ref, (y - j), rates, state), start)
    state = tuple(start[:, i * 128 : (i + 1) * 128] for i in range(width // 128))
    recur(maps_ref, codes_ref, drive_ref, rates, state, out)
    z, c = exp // CORES, exp % CORES

    def gate(j, carry):
        rows = pl.ds(pl.multiple_of(j * GROUP, GROUP), GROUP)
        away = (j // CORES + DEPTH - z) % DEPTH
        to = (j % CORES + c) % CORES * DEPTH + away % 2 * (DEPTH // 2) + away // 2
        value = out[rows, :] + skip_ref[...] * signal_ref[rows, :]
        arranged[pl.ds(pl.multiple_of(to * GROUP, GROUP), GROUP), :] = value * gate_ref[rows, :]
        return carry

    lax.fori_loop(0, codes_ref.shape[0] // GROUP, gate, 0)
    gated[...] = arranged[...].astype(BF16)
    fetch.wait()
    half = own_ref.shape[0]
    step = 512

    def product(k, carry):
        cols = pl.ds(pl.multiple_of(k * step, step), step)
        block = jnp.dot(gated[...], proj[:, cols], preferred_element_type=F32)
        own_ref[:, cols] = block[:half].astype(BF16)
        other_ref[:, cols] = block[half:].astype(BF16)
        return carry

    lax.fori_loop(0, proj.shape[1] // step, product, 0)


def state_space(
    inner_input, gate_input, step_codes, conv_weight, conv_bias, decay_rates, skip_gain, state_proj, out_proj
):
    length, width = inner_input.shape
    taps = conv_weight.shape[0]
    count = decay_rates.shape[0]
    model = out_proj.shape[1]
    border = shifted(inner_input[length - taps + 1 :], "ctx", 1)

    def wide(rows, kind=F32):
        return jax.ShapeDtypeStruct((rows, width), kind)

    maps_shape = jax.ShapeDtypeStruct((2 * count, length), F32)
    conv, codes, gate, taps_in, proj, rates, skip = pl.pallas_call(
        stage_kernel,
        out_shape=(
            wide(length), wide(length), wide(length), wide(taps), wide(2 * count, BF16), wide(count), wide(1),
        ),
        in_specs=[HBM] * 8,
        out_specs=(VMEM,) * 7,
        scratch_shapes=[
            pltpu.VMEM((length, width), BF16),
            pltpu.VMEM((length, width), jnp.int32),
            pltpu.VMEM((length, width), BF16),
            pltpu.VMEM((1, width), F32),
            pltpu.VMEM((count, width), F32),
            pltpu.VMEM((length + 8, width), F32),
            pltpu.SemaphoreType.DMA((8,)),
        ],
        compiler_params=SMALL,
        cost_estimate=pl.CostEstimate(flops=1 << 20, bytes_accessed=8 << 20, transcendentals=1 << 16),
        name="stage",
    )(
        *in_hbm(
            inner_input,
            step_codes,
            gate_input,
            conv_weight,
            conv_bias[None],
            state_proj.T,
            decay_rates,
            skip_gain[None],
        )
    )
    signal, drive, part = pl.pallas_call(
        signal_kernel,
        out_shape=(wide(length), wide(length), maps_shape),
        in_specs=[VMEM] * 5,
        out_specs=(VMEM,) * 3,
        compiler_params=SMALL,
        name="signal",
    )(border, conv, codes, taps_in, proj)
    part = sum(near(part), part)
    maps, sent = pl.pallas_call(
        end_kernel,
        out_shape=(maps_shape, wide(2 * count, BF16)),
        in_specs=[VMEM] * 7,
        out_specs=(VMEM,) * 2,
        compiler_params=SMALL,
        name="end_state",
    )(part, *far([part] * (DEPTH // 2)), codes, drive, rates)
    ends, line = pl.pallas_call(
        line_kernel,
        out_shape=(wide(2 * count * SIDE_Y, BF16), wide(2 * count, BF16)),
        in_specs=[VMEM] * 5,
        out_specs=(VMEM,) * 2,
        compiler_params=SMALL,
        name="line",
    )(sent, *[along_plane(sent, 0, k) for k in range(1, SIDE_Y)], rates)
    rows = join([line] + [along_plane(line, k, 0) for k in range(1, SIDE_X)])
    half = jax.ShapeDtypeStruct((length // 2, model), BF16)
    return pl.pallas_call(
        scan_kernel,
        out_shape=(half, half),
        in_specs=[VMEM] * 9 + [HBM],
        out_specs=(VMEM,) * 2,
        scratch_shapes=[
            pltpu.VMEM((length, width), F32),
            pltpu.VMEM((length, width), F32),
            pltpu.VMEM((length, width), BF16),
            pltpu.VMEM((width, model), BF16),
            pltpu.SemaphoreType.DMA,
        ],
        compiler_params=MEDIUM,
        name="scan",
    )(rows, ends, maps, codes, drive, signal, rates, skip, gate, *in_hbm(out_proj))


def join_kernel(*refs):
    out = refs[-1]
    at = 0
    for ref in refs[:-1]:
        out[at : at + ref.shape[0], :] = ref[...]
        at += ref.shape[0]


def join(arrays):
    rows = sum(a.shape[0] for a in arrays)
    return pl.pallas_call(
        join_kernel,
        out_shape=jax.ShapeDtypeStruct((rows,) + arrays[0].shape[1:], arrays[0].dtype),
        in_specs=[VMEM] * len(arrays),
        out_specs=VMEM,
        compiler_params=SMALL,
        name="join",
    )(*arrays)


def in_hbm(*arrays):
    return [pltpu.with_memory_space_constraint(a, pltpu.HBM) for a in arrays]


def added(*arrays):
    return sum(a.astype(F32) for a in arrays).astype(BF16)


def sum_out(own, other):
    pair = added(own, along_depth(other, lambda z, c: (z, 1 - c)))
    even, up, down = pair[: 4 * GROUP], pair[4 * GROUP : 6 * GROUP], pair[6 * GROUP :]
    low = split(along_depth(up, lambda z, c: (z + 1, c)), 2)
    high = split(along_depth(down, lambda z, c: (z - 1, c)), 2)
    even = split(even, 4)
    blocks = [added(even[0], low[0], high[1]), added(even[1], low[1]), even[2], added(even[3], high[0])]
    return sum((a.astype(F32) for a in far(blocks)), blocks[0].astype(F32))


def expert_kernel(count, *refs):
    pieces, (up_ref, down_ref), outs = refs[:count], refs[count : count + 2], refs[count + 2 : 2 * count + 2]
    rows, hidden = refs[2 * count + 2 :]
    step = 256
    places = []
    at = 0
    for ref in pieces:
        places.append(slice(at, at + ref.shape[0]))
        rows[places[-1], :] = ref[...]
        at += ref.shape[0]
    for k in range(up_ref.shape[1] // step):
        cols = slice(k * step, (k + 1) * step)
        block = jnp.dot(rows[...], up_ref[:, cols], preferred_element_type=F32)
        hidden[:, cols] = silu(block).astype(BF16)

    def down(k, carry):
        cols = pl.ds(pl.multiple_of(k * step, step), step)
        block = jnp.dot(hidden[...], down_ref[:, cols], preferred_element_type=F32).astype(BF16)
        for place, out in zip(places, outs):
            out[:, cols] = block[place]
        return carry

    lax.fori_loop(0, down_ref.shape[1] // step, down, 0)


def expert(pieces, up, down):
    size = sum(p.shape[0] for p in pieces)
    model, width = up.shape
    return pl.pallas_call(
        functools.partial(expert_kernel, len(pieces)),
        out_shape=tuple(jax.ShapeDtypeStruct(p.shape, BF16) for p in pieces),
        in_specs=[VMEM] * (len(pieces) + 2),
        out_specs=(VMEM,) * len(pieces),
        scratch_shapes=[pltpu.VMEM((size, model), BF16), pltpu.VMEM((size, width), BF16)],
        compiler_params=MEDIUM,
        cost_estimate=pl.CostEstimate(
            flops=4 * size * model * width, bytes_accessed=4 * size * model, transcendentals=size * width
        ),
        name="expert",
    )(*pieces, up, down)


def fetch_kernel(after_ref, up_ref, down_ref, up_out, down_out, sems):
    up = pltpu.make_async_copy(up_ref, up_out, sems.at[0])
    down = pltpu.make_async_copy(down_ref, down_out, sems.at[1])
    up.start()
    down.start()
    up.wait()
    down.wait()


def fetch(after, up, down):
    return pl.pallas_call(
        fetch_kernel,
        out_shape=(jax.ShapeDtypeStruct(up.shape, BF16), jax.ShapeDtypeStruct(down.shape, BF16)),
        in_specs=[pl.BlockSpec(memory_space=pl.ANY), HBM, HBM],
        out_specs=(VMEM, VMEM),
        scratch_shapes=[pltpu.SemaphoreType.DMA((2,))],
        compiler_params=SMALL,
        cost_estimate=pl.CostEstimate(flops=0, bytes_accessed=32 << 20, transcendentals=0),
        name="fetch",
    )(after, *in_hbm(up, down))


def split(array, parts):
    size = array.shape[0] // parts
    return [array[k * size : (k + 1) * size] for k in range(parts)]


def swap(array):
    return along_depth(array, lambda z, c: (z, 1 - c))


def along_side(array, side, step):
    pairs = []
    for x in range(SIDE_X):
        for y in range(SIDE_Y):
            for exp in range(DEPTH * CORES):
                if (side + exp) % 2 == 0:
                    to = (x + step) % SIDE_X * SIDE_Y + y
                else:
                    to = x * SIDE_Y + (y + step) % SIDE_Y
                pairs.append(((x * SIDE_Y + y) * DEPTH * CORES + exp, to * DEPTH * CORES + exp))
    return lax.ppermute(array, ("ctx", "exp"), pairs)


def run_expert(mine, theirs, up, down):
    steps = (1, 2, 3)
    base = jnp.concatenate([mine, theirs])
    size = mine.shape[0]
    visits = [base] + [along_side(base, 0, k) for k in steps]
    group = join([v[:size] for v in visits] + [v[size:] for v in visits])
    half = group.shape[0] // 2
    after, before = along_side(group, 1, 1), along_side(group, 1, -1)
    up, down = fetch(group, up, down)
    own_mine, own_swapped = expert([group[:half], swap(group[half:])], up, down)
    after, before, up, down, own_mine, own_swapped = lax.optimization_barrier(
        (after, before, up, down, own_mine, own_swapped)
    )
    far_mine = along_side(after[:half], 1, 1)
    far_theirs = along_side(before[half:], 1, -1)
    close = [after[:half], before[:half], swap(after[half:]), swap(before[half:])]
    far_mine, far_swapped = expert([far_mine, swap(far_theirs)], up, down)
    passed = along_side(far_mine, 1, -1), along_side(swap(far_swapped), 1, 1)
    after_mine, before_mine, after_swapped, before_swapped = expert(close, up, down)
    own_theirs, after_theirs, before_theirs = swap(own_swapped), swap(after_swapped), swap(before_swapped)
    one = along_side(jnp.concatenate([added(after_mine, passed[0]), after_theirs]), 1, -1)
    three = along_side(jnp.concatenate([before_mine, added(before_theirs, passed[1])]), 1, 1)
    total_mine = split(added(own_mine, one[:half], three[:half]), 4)
    total_theirs = split(added(own_theirs, one[half:], three[half:]), 4)
    blocks = [jnp.concatenate([m, t]) for m, t in zip(total_mine, total_theirs)]
    return added(blocks[0], *[along_side(blocks[k], 0, -k) for k in steps])


def shards(
    inner_input,
    gate_input,
    step_codes,
    conv_weight,
    conv_bias,
    decay_rates,
    skip_gain,
    state_proj,
    out_proj,
    residual,
    norm_gain,
    expert_ids,
    gate_codes,
    up_weight,
    down_weight,
):
    own, other = state_space(
        inner_input,
        gate_input,
        step_codes,
        conv_weight,
        conv_bias,
        decay_rates,
        skip_gain,
        state_proj,
        out_proj,
    )
    row_count = residual.shape[0]
    mamba_out = sum_out(own, other)
    stream = (residual.astype(F32) + mamba_out).astype(BF16)
    stream_wide = stream.astype(F32)
    normed = (
        stream_wide
        * lax.rsqrt(jnp.mean(stream_wide * stream_wide, axis=-1, keepdims=True) + 1e-05)
        * norm_gain
    ).astype(BF16)
    experts = lax.axis_size("exp") * up_weight.shape[0]
    top_count = expert_ids.shape[1]
    capacity = max(2, 4 * row_count // experts)
    onehot = (
        (expert_ids[:, :, None] == jnp.arange(experts)[None, None, :])
        .astype(jnp.int32)
        .reshape(row_count * top_count, experts)
    )
    before = jnp.cumsum(onehot, axis=0) - onehot
    ranking = jnp.sum(before * onehot, axis=1).reshape(row_count, top_count)
    slot_index = expert_ids // CORES * (CORES * capacity) + ranking * CORES
    slot_index = slot_index + (expert_ids % CORES != ranking).astype(jnp.int32)
    slots = slot_index[:, :, None] == jnp.arange(experts * capacity)[None, None, :]
    dispatch_table = jnp.any(slots, axis=1).astype(BF16)
    up_local = up_weight[0]
    down_local = down_weight[0]
    outgoing = lax.dot_general(
        dispatch_table, normed, (((0,), (0,)), ((), ())), preferred_element_type=F32
    ).astype(BF16)
    outgoing = outgoing.reshape(experts, capacity, -1)
    arrived = lax.all_to_all(outgoing, "exp", split_axis=0, concat_axis=0, tiled=True)
    expert_out = run_expert(arrived[:, 0], arrived[:, 1], up_local, down_local)
    expert_out = jnp.stack(split(expert_out, 2), axis=1)
    returned = lax.all_to_all(expert_out, "exp", split_axis=0, concat_axis=0, tiled=True)
    returned = returned.reshape(experts * capacity, -1)
    gate_weights = gate_codes.astype(F32)
    gate_weights = gate_weights / jnp.sum(gate_weights, axis=1, keepdims=True)
    table = jnp.sum(gate_weights[:, :, None] * slots.astype(F32), axis=1)
    mixture_out = jnp.dot(table, returned.astype(F32), precision=lax.Precision.HIGHEST)
    return (stream_wide + mixture_out).astype(BF16)


def solution(mesh):
    return jax.shard_map(
        shards,
        mesh=mesh,
        in_specs=(
            P("ctx", "exp"),
            P("ctx", "exp"),
            P("ctx", "exp"),
            P(None, "exp"),
            P("exp"),
            P(None, "exp"),
            P("exp"),
            P("exp", None),
            P("exp", None),
            P(("ctx", "exp"), None),
            P(),
            P(("ctx", "exp"), None),
            P(("ctx", "exp"), None),
            P("exp", None, "ctx"),
            P("exp", "ctx", None),
        ),
        out_specs=P(("ctx", "exp"), None),
        check_vma=False,
    )
```

```python
import functools
import math
import jax
import jax.numpy as jnp
from jax import lax
from jax.experimental import pallas as pl
from jax.experimental.pallas import tpu as pltpu
from jax.sharding import PartitionSpec as P

F32 = jnp.float32
BF16 = jnp.bfloat16
SIDE_X, SIDE_Y = 4, 4
DEPTH, CORES = 8, 2
GROUP = 8
SPAN = 32
VMEM = pl.BlockSpec(memory_space=pltpu.VMEM)
HBM = pl.BlockSpec(memory_space=pltpu.HBM)
SMALL = pltpu.CompilerParams(vmem_limit_bytes=8 * 1024 * 1024)
MEDIUM = pltpu.CompilerParams(vmem_limit_bytes=20 * 1024 * 1024)


def shifted(array, axis, by):
    count = lax.axis_size(axis)
    pairs = [(i, i + by) for i in range(count) if 0 <= i + by < count]
    return lax.ppermute(array, axis, pairs)


def along_plane(array, dx, dy):
    pairs = [
        (x * SIDE_Y + y, (x + dx) % SIDE_X * SIDE_Y + (y + dy) % SIDE_Y)
        for x in range(SIDE_X)
        for y in range(SIDE_Y)
    ]
    return lax.ppermute(array, "ctx", pairs)


def along_depth(array, target):
    pairs = []
    for z in range(DEPTH):
        for c in range(CORES):
            to_z, to_c = target(z, c)
            pairs.append((z * CORES + c, to_z % DEPTH * CORES + to_c))
    return lax.ppermute(array, "exp", pairs)


def near(array):
    return [
        along_depth(array, lambda z, c: (z, 1 - c)),
        along_depth(array, lambda z, c: (z ^ 1, c)),
        along_depth(array, lambda z, c: (z ^ 1, 1 - c)),
    ]


def far(arrays):
    return [along_depth(a, lambda z, c, k=k: (z + 2 * k, c)) for k, a in enumerate(arrays) if k]


def silu(v):
    return v / (1.0 + jnp.exp(-v))


def stage_kernel(
    inner_ref, codes_ref, gate_ref, taps_ref, bias_ref, proj_ref, rates_ref, skip_ref,
    conv_out, codes_out, gate_out, taps_out, proj_out, rates_out, skip_out,
    inner, codes, gate, bias, rates, padded, sems,
):
    moves = [
        (inner_ref, inner),
        (taps_ref, taps_out),
        (bias_ref, bias),
        (codes_ref, codes),
        (gate_ref, gate),
        (proj_ref, proj_out),
        (rates_ref, rates),
        (skip_ref, skip_out),
    ]
    copies = [pltpu.make_async_copy(a, b, sems.at[k]) for k, (a, b) in enumerate(moves)]
    for copy in copies:
        copy.start()
    length = inner.shape[0]
    count = taps_out.shape[0]
    padded[0:8, :] = jnp.zeros((8, padded.shape[1]), F32)
    for copy in copies[:3]:
        copy.wait()
    padded[8:, :] = inner[...].astype(F32)
    total = taps_out[0:1, :] * padded[8 - count + 1 : 8 - count + 1 + length, :]
    for k in range(1, count):
        start = 8 - count + 1 + k
        total = total + taps_out[k : k + 1, :] * padded[start : start + length, :]
    conv_out[...] = total + bias[...]
    for copy in copies[3:]:
        copy.wait()
    codes_out[...] = codes[...].astype(F32)
    gate_out[...] = silu(gate[...].astype(F32))
    rates_out[...] = rates[...] * (-math.log2(math.e) / 256.0)


def signal_kernel(border_ref, conv_ref, codes_ref, taps_ref, proj_ref, signal_ref, drive_ref, maps_ref):
    count = taps_ref.shape[0]
    width = conv_ref.shape[1]
    border = border_ref[...].astype(F32)
    rows = lax.broadcasted_iota(jnp.int32, (8, width), 0)
    first = jnp.zeros((8, width), F32)
    for t in range(count - 1):
        row = jnp.zeros((1, width), F32)
        for k in range(count - 1 - t):
            row = row + taps_ref[k : k + 1, :] * border[t + k : t + k + 1, :]
        first = jnp.where(rows == t, row, first)
    signal_ref[...] = silu(conv_ref[...])
    signal_ref[0:8, :] = silu(conv_ref[0:8, :] + first)
    signal = signal_ref[...]
    drive_ref[...] = jnp.minimum(codes_ref[...] * (1.0 / 256.0), 1.0) * signal
    maps_ref[...] = lax.dot_general(
        proj_ref[...],
        signal.astype(BF16),
        (((1,), (1,)), ((), ())),
        preferred_element_type=F32,
    )


def recur(maps_ref, codes_ref, drive_ref, rates, state, out_ref):
    width = codes_ref.shape[1]
    count = rates.shape[0]
    tiles = width // 128

    def group(g, state):
        rows = pl.ds(pl.multiple_of(g * SPAN, SPAN), SPAN)
        codes = codes_ref[rows, :]
        drive = drive_ref[rows, :]
        lanes = maps_ref.shape[1]
        maps = pltpu.roll(maps_ref[...], (lanes - g * SPAN) % lanes, 1)
        outs = []
        for k in range(SPAN):
            into = jnp.broadcast_to(maps[:count, k : k + 1], (count, 128))
            if out_ref is not None:
                out_of = jnp.broadcast_to(maps[count:, k : k + 1], (count, 128))
            pieces = []
            new = []
            for i in range(tiles):
                cols = slice(i * 128, (i + 1) * 128)
                decay = jnp.exp2(codes[k : k + 1, cols] * rates[:, cols])
                now = decay * state[i] + into * drive[k : k + 1, cols]
                new.append(now)
                if out_ref is not None:
                    pieces.append(jnp.sum(out_of * now, axis=0, keepdims=True))
            state = tuple(new)
            if out_ref is not None:
                outs.append(jnp.concatenate(pieces, axis=1))
        if out_ref is not None:
            out_ref[rows, :] = jnp.concatenate(outs, axis=0)
        return state

    return lax.fori_loop(0, codes_ref.shape[0] // SPAN, group, state)


def end_kernel(a_ref, b_ref, c_ref, d_ref, codes_ref, drive_ref, rates_ref, maps_ref, sent_ref):
    maps_ref[...] = (a_ref[...] + b_ref[...]) + (c_ref[...] + d_ref[...])
    rates = rates_ref[...]
    count, width = rates.shape
    zero = tuple(jnp.zeros((count, 128), F32) for _ in range(width // 128))
    state = jnp.concatenate(recur(maps_ref, codes_ref, drive_ref, rates, zero, None), axis=1)
    sent_ref[...] = packed(state, jnp.sum(codes_ref[...], axis=0, keepdims=True))


def packed(state, total):
    rows = lax.broadcasted_iota(jnp.int32, state.shape, 0)
    parts = jnp.zeros(state.shape, F32)
    for i in range(3):
        part = total.astype(BF16).astype(F32)
        parts = jnp.where(rows == i, part, parts)
        total = total - part
    return jnp.concatenate([state, parts], axis=0).astype(BF16)


def unpacked(ref, k, count):
    block = ref[pl.ds(pl.multiple_of(k * 2 * count, 2 * count), 2 * count), :].astype(F32)
    return block[:count], block[count : count + 1] + block[count + 1 : count + 2] + block[count + 2 : count + 3]


def follow(ref, k, rates, state):
    end, total = unpacked(ref, k, rates.shape[0])
    return jnp.exp2(total * rates) * state + end


def line_kernel(a_ref, b_ref, c_ref, d_ref, rates_ref, ends_ref, sent_ref):
    rates = rates_ref[...]
    count, width = rates.shape
    for k, ref in enumerate((a_ref, b_ref, c_ref, d_ref)):
        ends_ref[2 * count * k : 2 * count * (k + 1), :] = ref[...]
    y = lax.axis_index("ctx") % SIDE_Y

    def one(j, carry):
        state, total = carry
        at = (y + SIDE_Y - j) % SIDE_Y
        end, more = unpacked(ends_ref, at, count)
        return jnp.exp2(more * rates) * state + end, total + more

    state, total = lax.fori_loop(
        0, SIDE_Y, one, (jnp.zeros((count, width), F32), jnp.zeros((1, width), F32))
    )
    sent_ref[...] = packed(state, total)


def scan_kernel(
    rows_ref, ends_ref, maps_ref, codes_ref, drive_ref, signal_ref, rates_ref, skip_ref, gate_ref, proj_ref,
    own_ref, other_ref, out, arranged, gated, proj, sem,
):
    fetch = pltpu.make_async_copy(proj_ref, proj, sem)
    fetch.start()
    rates = rates_ref[...]
    count, width = rates.shape
    ctx, exp = lax.axis_index("ctx"), lax.axis_index("exp")
    x, y = ctx // SIDE_Y, ctx % SIDE_Y

    zero = jnp.zeros((count, width), F32)
    start = lax.fori_loop(0, x, lambda j, state: follow(rows_ref, (x - j), rates, state), zero)
    start = lax.fori_loop(0, y, lambda j, state: follow(ends_ref, (y - j), rates, state), start)
    state = tuple(start[:, i * 128 : (i + 1) * 128] for i in range(width // 128))
    recur(maps_ref, codes_ref, drive_ref, rates, state, out)
    z, c = exp // CORES, exp % CORES

    def gate(j, carry):
        rows = pl.ds(pl.multiple_of(j * GROUP, GROUP), GROUP)
        away = (j // CORES + DEPTH - z) % DEPTH
        to = (j % CORES + c) % CORES * DEPTH + away % 2 * (DEPTH // 2) + away // 2
        value = out[rows, :] + skip_ref[...] * signal_ref[rows, :]
        arranged[pl.ds(pl.multiple_of(to * GROUP, GROUP), GROUP), :] = value * gate_ref[rows, :]
        return carry

    lax.fori_loop(0, codes_ref.shape[0] // GROUP, gate, 0)
    gated[...] = arranged[...].astype(BF16)
    fetch.wait()
    half = own_ref.shape[0]
    step = 512

    def product(k, carry):
        cols = pl.ds(pl.multiple_of(k * step, step), step)
        block = jnp.dot(gated[...], proj[:, cols], preferred_element_type=F32)
        own_ref[:, cols] = block[:half].astype(BF16)
        other_ref[:, cols] = block[half:].astype(BF16)
        return carry

    lax.fori_loop(0, proj.shape[1] // step, product, 0)


def state_space(
    inner_input, gate_input, step_codes, conv_weight, conv_bias, decay_rates, skip_gain, state_proj, out_proj
):
    length, width = inner_input.shape
    taps = conv_weight.shape[0]
    count = decay_rates.shape[0]
    model = out_proj.shape[1]
    border = shifted(inner_input[length - taps + 1 :], "ctx", 1)

    def wide(rows, kind=F32):
        return jax.ShapeDtypeStruct((rows, width), kind)

    maps_shape = jax.ShapeDtypeStruct((2 * count, length), F32)
    conv, codes, gate, taps_in, proj, rates, skip = pl.pallas_call(
        stage_kernel,
        out_shape=(
            wide(length), wide(length), wide(length), wide(taps), wide(2 * count, BF16), wide(count), wide(1),
        ),
        in_specs=[HBM] * 8,
        out_specs=(VMEM,) * 7,
        scratch_shapes=[
            pltpu.VMEM((length, width), BF16),
            pltpu.VMEM((length, width), jnp.int32),
            pltpu.VMEM((length, width), BF16),
            pltpu.VMEM((1, width), F32),
            pltpu.VMEM((count, width), F32),
            pltpu.VMEM((length + 8, width), F32),
            pltpu.SemaphoreType.DMA((8,)),
        ],
        compiler_params=SMALL,
        cost_estimate=pl.CostEstimate(flops=1 << 20, bytes_accessed=8 << 20, transcendentals=1 << 16),
        name="stage",
    )(
        *in_hbm(
            inner_input,
            step_codes,
            gate_input,
            conv_weight,
            conv_bias[None],
            state_proj.T,
            decay_rates,
            skip_gain[None],
        )
    )
    signal, drive, part = pl.pallas_call(
        signal_kernel,
        out_shape=(wide(length), wide(length), maps_shape),
        in_specs=[VMEM] * 5,
        out_specs=(VMEM,) * 3,
        compiler_params=SMALL,
        name="signal",
    )(border, conv, codes, taps_in, proj)
    part = sum(near(part), part)
    maps, sent = pl.pallas_call(
        end_kernel,
        out_shape=(maps_shape, wide(2 * count, BF16)),
        in_specs=[VMEM] * 7,
        out_specs=(VMEM,) * 2,
        compiler_params=SMALL,
        name="end_state",
    )(part, *far([part] * (DEPTH // 2)), codes, drive, rates)
    ends, line = pl.pallas_call(
        line_kernel,
        out_shape=(wide(2 * count * SIDE_Y, BF16), wide(2 * count, BF16)),
        in_specs=[VMEM] * 5,
        out_specs=(VMEM,) * 2,
        compiler_params=SMALL,
        name="line",
    )(sent, *[along_plane(sent, 0, k) for k in range(1, SIDE_Y)], rates)
    rows = join([line] + [along_plane(line, k, 0) for k in range(1, SIDE_X)])
    half = jax.ShapeDtypeStruct((length // 2, model), BF16)
    return pl.pallas_call(
        scan_kernel,
        out_shape=(half, half),
        in_specs=[VMEM] * 9 + [HBM],
        out_specs=(VMEM,) * 2,
        scratch_shapes=[
            pltpu.VMEM((length, width), F32),
            pltpu.VMEM((length, width), F32),
            pltpu.VMEM((length, width), BF16),
            pltpu.VMEM((width, model), BF16),
            pltpu.SemaphoreType.DMA,
        ],
        compiler_params=MEDIUM,
        name="scan",
    )(rows, ends, maps, codes, drive, signal, rates, skip, gate, *in_hbm(out_proj))


def join_kernel(*refs):
    out = refs[-1]
    at = 0
    for ref in refs[:-1]:
        out[at : at + ref.shape[0], :] = ref[...]
        at += ref.shape[0]


def join(arrays):
    rows = sum(a.shape[0] for a in arrays)
    return pl.pallas_call(
        join_kernel,
        out_shape=jax.ShapeDtypeStruct((rows,) + arrays[0].shape[1:], arrays[0].dtype),
        in_specs=[VMEM] * len(arrays),
        out_specs=VMEM,
        compiler_params=SMALL,
        name="join",
    )(*arrays)


def in_hbm(*arrays):
    return [pltpu.with_memory_space_constraint(a, pltpu.HBM) for a in arrays]


def added(*arrays):
    return sum(a.astype(F32) for a in arrays).astype(BF16)


def sum_out(own, other):
    pair = added(own, along_depth(other, lambda z, c: (z, 1 - c)))
    even, up, down = pair[: 4 * GROUP], pair[4 * GROUP : 6 * GROUP], pair[6 * GROUP :]
    low = split(along_depth(up, lambda z, c: (z + 1, c)), 2)
    high = split(along_depth(down, lambda z, c: (z - 1, c)), 2)
    even = split(even, 4)
    blocks = [added(even[0], low[0], high[1]), added(even[1], low[1]), even[2], added(even[3], high[0])]
    return sum((a.astype(F32) for a in far(blocks)), blocks[0].astype(F32))


def expert_kernel(count, *refs):
    pieces, (up_ref, down_ref), outs = refs[:count], refs[count : count + 2], refs[count + 2 : 2 * count + 2]
    rows, hidden = refs[2 * count + 2 :]
    step = 256
    places = []
    at = 0
    for ref in pieces:
        places.append(slice(at, at + ref.shape[0]))
        rows[places[-1], :] = ref[...]
        at += ref.shape[0]
    for k in range(up_ref.shape[1] // step):
        cols = slice(k * step, (k + 1) * step)
        block = jnp.dot(rows[...], up_ref[:, cols], preferred_element_type=F32)
        hidden[:, cols] = silu(block).astype(BF16)

    def down(k, carry):
        cols = pl.ds(pl.multiple_of(k * step, step), step)
        block = jnp.dot(hidden[...], down_ref[:, cols], preferred_element_type=F32).astype(BF16)
        for place, out in zip(places, outs):
            out[:, cols] = block[place]
        return carry

    lax.fori_loop(0, down_ref.shape[1] // step, down, 0)


def expert(pieces, up, down):
    size = sum(p.shape[0] for p in pieces)
    model, width = up.shape
    return pl.pallas_call(
        functools.partial(expert_kernel, len(pieces)),
        out_shape=tuple(jax.ShapeDtypeStruct(p.shape, BF16) for p in pieces),
        in_specs=[VMEM] * (len(pieces) + 2),
        out_specs=(VMEM,) * len(pieces),
        scratch_shapes=[pltpu.VMEM((size, model), BF16), pltpu.VMEM((size, width), BF16)],
        compiler_params=MEDIUM,
        cost_estimate=pl.CostEstimate(
            flops=4 * size * model * width, bytes_accessed=4 * size * model, transcendentals=size * width
        ),
        name="expert",
    )(*pieces, up, down)


def fetch_kernel(after_ref, up_ref, down_ref, up_out, down_out, sems):
    up = pltpu.make_async_copy(up_ref, up_out, sems.at[0])
    down = pltpu.make_async_copy(down_ref, down_out, sems.at[1])
    up.start()
    down.start()
    up.wait()
    down.wait()


def fetch(after, up, down):
    return pl.pallas_call(
        fetch_kernel,
        out_shape=(jax.ShapeDtypeStruct(up.shape, BF16), jax.ShapeDtypeStruct(down.shape, BF16)),
        in_specs=[pl.BlockSpec(memory_space=pl.ANY), HBM, HBM],
        out_specs=(VMEM, VMEM),
        scratch_shapes=[pltpu.SemaphoreType.DMA((2,))],
        compiler_params=SMALL,
        cost_estimate=pl.CostEstimate(flops=0, bytes_accessed=32 << 20, transcendentals=0),
        name="fetch",
    )(after, *in_hbm(up, down))


def split(array, parts):
    size = array.shape[0] // parts
    return [array[k * size : (k + 1) * size] for k in range(parts)]


def swap(array):
    return along_depth(array, lambda z, c: (z, 1 - c))


def along_side(array, side, step):
    pairs = []
    for x in range(SIDE_X):
        for y in range(SIDE_Y):
            for exp in range(DEPTH * CORES):
                if (side + exp) % 2 == 0:
                    to = (x + step) % SIDE_X * SIDE_Y + y
                else:
                    to = x * SIDE_Y + (y + step) % SIDE_Y
                pairs.append(((x * SIDE_Y + y) * DEPTH * CORES + exp, to * DEPTH * CORES + exp))
    return lax.ppermute(array, ("ctx", "exp"), pairs)


def run_expert(mine, theirs, up, down):
    steps = (1, 2, 3)
    base = jnp.concatenate([mine, theirs])
    size = mine.shape[0]
    visits = [base] + [along_side(base, 0, k) for k in steps]
    group = join([v[:size] for v in visits] + [v[size:] for v in visits])
    half = group.shape[0] // 2
    before_theirs = along_side(group[half:], 1, -1)
    after, before_mine = along_side(group, 1, 1), along_side(group[:half], 1, -1)
    up, down = fetch(group, up, down)
    own_mine, own_swapped = expert([group[:half], swap(group[half:])], up, down)
    after, before_mine, up, down, own_mine, own_swapped = lax.optimization_barrier(
        (after, before_mine, up, down, own_mine, own_swapped)
    )
    before_swapped = swap(before_theirs)
    far_mine, far_swapped = along_side(after[:half], 1, 1), along_side(before_swapped, 0, -1)
    close = [after[:half], before_mine, swap(after[half:]), before_swapped]
    far_mine, far_swapped = expert([far_mine, far_swapped], up, down)
    passed_mine, passed_swapped = along_side(far_mine, 1, -1), along_side(far_swapped, 0, 1)
    passed_mine, passed_swapped = lax.optimization_barrier((passed_mine, passed_swapped))
    after_mine, before_mine, after_swapped, before_swapped = expert(close, up, down)
    own_theirs, after_theirs = swap(own_swapped), swap(after_swapped)
    before_theirs = swap(added(before_swapped, passed_swapped))
    one = along_side(jnp.concatenate([added(after_mine, passed_mine), after_theirs]), 1, -1)
    three_mine, three_theirs = along_side(before_mine, 1, 1), along_side(before_theirs, 1, 1)
    total_mine = split(added(own_mine, one[:half], three_mine), 4)
    total_theirs = split(added(own_theirs, one[half:], three_theirs), 4)
    blocks = [jnp.concatenate([m, t]) for m, t in zip(total_mine, total_theirs)]
    return added(blocks[0], *[along_side(blocks[k], 0, -k) for k in steps])


def shards(
    inner_input,
    gate_input,
    step_codes,
    conv_weight,
    conv_bias,
    decay_rates,
    skip_gain,
    state_proj,
    out_proj,
    residual,
    norm_gain,
    expert_ids,
    gate_codes,
    up_weight,
    down_weight,
):
    own, other = state_space(
        inner_input,
        gate_input,
        step_codes,
        conv_weight,
        conv_bias,
        decay_rates,
        skip_gain,
        state_proj,
        out_proj,
    )
    row_count = residual.shape[0]
    mamba_out = sum_out(own, other)
    stream = (residual.astype(F32) + mamba_out).astype(BF16)
    stream_wide = stream.astype(F32)
    normed = (
        stream_wide
        * lax.rsqrt(jnp.mean(stream_wide * stream_wide, axis=-1, keepdims=True) + 1e-05)
        * norm_gain
    ).astype(BF16)
    experts = lax.axis_size("exp") * up_weight.shape[0]
    top_count = expert_ids.shape[1]
    capacity = max(2, 4 * row_count // experts)
    onehot = (
        (expert_ids[:, :, None] == jnp.arange(experts)[None, None, :])
        .astype(jnp.int32)
        .reshape(row_count * top_count, experts)
    )
    before = jnp.cumsum(onehot, axis=0) - onehot
    ranking = jnp.sum(before * onehot, axis=1).reshape(row_count, top_count)
    slot_index = expert_ids // CORES * (CORES * capacity) + ranking * CORES
    slot_index = slot_index + (expert_ids % CORES != ranking).astype(jnp.int32)
    slots = slot_index[:, :, None] == jnp.arange(experts * capacity)[None, None, :]
    dispatch_table = jnp.any(slots, axis=1).astype(BF16)
    up_local = up_weight[0]
    down_local = down_weight[0]
    outgoing = lax.dot_general(
        dispatch_table, normed, (((0,), (0,)), ((), ())), preferred_element_type=F32
    ).astype(BF16)
    outgoing = outgoing.reshape(experts, capacity, -1)
    arrived = lax.all_to_all(outgoing, "exp", split_axis=0, concat_axis=0, tiled=True)
    expert_out = run_expert(arrived[:, 0], arrived[:, 1], up_local, down_local)
    expert_out = jnp.stack(split(expert_out, 2), axis=1)
    returned = lax.all_to_all(expert_out, "exp", split_axis=0, concat_axis=0, tiled=True)
    returned = returned.reshape(experts * capacity, -1)
    gate_weights = gate_codes.astype(F32)
    gate_weights = gate_weights / jnp.sum(gate_weights, axis=1, keepdims=True)
    table = jnp.sum(gate_weights[:, :, None] * slots.astype(F32), axis=1)
    mixture_out = jnp.dot(table, returned.astype(F32), precision=lax.Precision.HIGHEST)
    return (stream_wide + mixture_out).astype(BF16)


def solution(mesh):
    return jax.shard_map(
        shards,
        mesh=mesh,
        in_specs=(
            P("ctx", "exp"),
            P("ctx", "exp"),
            P("ctx", "exp"),
            P(None, "exp"),
            P("exp"),
            P(None, "exp"),
            P("exp"),
            P("exp", None),
            P("exp", None),
            P(("ctx", "exp"), None),
            P(),
            P(("ctx", "exp"), None),
            P(("ctx", "exp"), None),
            P("exp", None, "ctx"),
            P("exp", "ctx", None),
        ),
        out_specs=P(("ctx", "exp"), None),
        check_vma=False,
    )
```

```python
import functools
import math
import jax
import jax.numpy as jnp
from jax import lax
from jax.experimental import pallas as pl
from jax.experimental.pallas import tpu as pltpu
from jax.sharding import PartitionSpec as P

F32 = jnp.float32
BF16 = jnp.bfloat16
SIDE_X, SIDE_Y = 4, 4
DEPTH, CORES = 8, 2
GROUP = 8
SPAN = 32
VMEM = pl.BlockSpec(memory_space=pltpu.VMEM)
HBM = pl.BlockSpec(memory_space=pltpu.HBM)
SMALL = pltpu.CompilerParams(vmem_limit_bytes=8 * 1024 * 1024)
MEDIUM = pltpu.CompilerParams(vmem_limit_bytes=20 * 1024 * 1024)


def shifted(array, axis, by):
    count = lax.axis_size(axis)
    pairs = [(i, i + by) for i in range(count) if 0 <= i + by < count]
    return lax.ppermute(array, axis, pairs)


def along_plane(array, dx, dy):
    pairs = [
        (x * SIDE_Y + y, (x + dx) % SIDE_X * SIDE_Y + (y + dy) % SIDE_Y)
        for x in range(SIDE_X)
        for y in range(SIDE_Y)
    ]
    return lax.ppermute(array, "ctx", pairs)


def along_depth(array, target):
    pairs = []
    for z in range(DEPTH):
        for c in range(CORES):
            to_z, to_c = target(z, c)
            pairs.append((z * CORES + c, to_z % DEPTH * CORES + to_c))
    return lax.ppermute(array, "exp", pairs)


def near(array):
    return [
        along_depth(array, lambda z, c: (z, 1 - c)),
        along_depth(array, lambda z, c: (z ^ 1, c)),
        along_depth(array, lambda z, c: (z ^ 1, 1 - c)),
    ]


def far(arrays):
    return [along_depth(a, lambda z, c, k=k: (z + 2 * k, c)) for k, a in enumerate(arrays) if k]


def silu(v):
    return v / (1.0 + jnp.exp(-v))


def stage_kernel(
    inner_ref, codes_ref, gate_ref, taps_ref, bias_ref, proj_ref, rates_ref, skip_ref,
    conv_out, codes_out, gate_out, taps_out, proj_out, rates_out, skip_out,
    inner, codes, gate, bias, rates, padded, sems,
):
    moves = [
        (inner_ref, inner),
        (taps_ref, taps_out),
        (bias_ref, bias),
        (codes_ref, codes),
        (gate_ref, gate),
        (proj_ref, proj_out),
        (rates_ref, rates),
        (skip_ref, skip_out),
    ]
    copies = [pltpu.make_async_copy(a, b, sems.at[k]) for k, (a, b) in enumerate(moves)]
    for copy in copies:
        copy.start()
    length = inner.shape[0]
    count = taps_out.shape[0]
    padded[0:8, :] = jnp.zeros((8, padded.shape[1]), F32)
    for copy in copies[:3]:
        copy.wait()
    padded[8:, :] = inner[...].astype(F32)
    total = taps_out[0:1, :] * padded[8 - count + 1 : 8 - count + 1 + length, :]
    for k in range(1, count):
        start = 8 - count + 1 + k
        total = total + taps_out[k : k + 1, :] * padded[start : start + length, :]
    conv_out[...] = total + bias[...]
    for copy in copies[3:]:
        copy.wait()
    codes_out[...] = codes[...].astype(F32)
    gate_out[...] = silu(gate[...].astype(F32))
    rates_out[...] = rates[...] * (-math.log2(math.e) / 256.0)


def signal_kernel(border_ref, conv_ref, codes_ref, taps_ref, proj_ref, signal_ref, drive_ref, maps_ref):
    count = taps_ref.shape[0]
    width = conv_ref.shape[1]
    border = border_ref[...].astype(F32)
    rows = lax.broadcasted_iota(jnp.int32, (8, width), 0)
    first = jnp.zeros((8, width), F32)
    for t in range(count - 1):
        row = jnp.zeros((1, width), F32)
        for k in range(count - 1 - t):
            row = row + taps_ref[k : k + 1, :] * border[t + k : t + k + 1, :]
        first = jnp.where(rows == t, row, first)
    signal_ref[...] = silu(conv_ref[...])
    signal_ref[0:8, :] = silu(conv_ref[0:8, :] + first)
    signal = signal_ref[...]
    drive_ref[...] = jnp.minimum(codes_ref[...] * (1.0 / 256.0), 1.0) * signal
    maps_ref[...] = lax.dot_general(
        proj_ref[...],
        signal.astype(BF16),
        (((1,), (1,)), ((), ())),
        preferred_element_type=F32,
    )


def recur(maps_ref, codes_ref, drive_ref, rates, state, out_ref):
    width = codes_ref.shape[1]
    count = rates.shape[0]
    tiles = width // 128

    def group(g, state):
        rows = pl.ds(pl.multiple_of(g * SPAN, SPAN), SPAN)
        codes = codes_ref[rows, :]
        drive = drive_ref[rows, :]
        lanes = maps_ref.shape[1]
        maps = pltpu.roll(maps_ref[...], (lanes - g * SPAN) % lanes, 1)
        outs = []
        for k in range(SPAN):
            into = jnp.broadcast_to(maps[:count, k : k + 1], (count, 128))
            if out_ref is not None:
                out_of = jnp.broadcast_to(maps[count:, k : k + 1], (count, 128))
            pieces = []
            new = []
            for i in range(tiles):
                cols = slice(i * 128, (i + 1) * 128)
                decay = jnp.exp2(codes[k : k + 1, cols] * rates[:, cols])
                now = decay * state[i] + into * drive[k : k + 1, cols]
                new.append(now)
                if out_ref is not None:
                    pieces.append(jnp.sum(out_of * now, axis=0, keepdims=True))
            state = tuple(new)
            if out_ref is not None:
                outs.append(jnp.concatenate(pieces, axis=1))
        if out_ref is not None:
            out_ref[rows, :] = jnp.concatenate(outs, axis=0)
        return state

    return lax.fori_loop(0, codes_ref.shape[0] // SPAN, group, state)


def end_kernel(a_ref, b_ref, c_ref, d_ref, codes_ref, drive_ref, rates_ref, maps_ref, sent_ref):
    maps_ref[...] = (a_ref[...] + b_ref[...]) + (c_ref[...] + d_ref[...])
    rates = rates_ref[...]
    count, width = rates.shape
    zero = tuple(jnp.zeros((count, 128), F32) for _ in range(width // 128))
    state = jnp.concatenate(recur(maps_ref, codes_ref, drive_ref, rates, zero, None), axis=1)
    sent_ref[...] = packed(state, jnp.sum(codes_ref[...], axis=0, keepdims=True))


def packed(state, total):
    rows = lax.broadcasted_iota(jnp.int32, state.shape, 0)
    parts = jnp.zeros(state.shape, F32)
    for i in range(3):
        part = total.astype(BF16).astype(F32)
        parts = jnp.where(rows == i, part, parts)
        total = total - part
    return jnp.concatenate([state, parts], axis=0).astype(BF16)


def unpacked(ref, k, count):
    block = ref[pl.ds(pl.multiple_of(k * 2 * count, 2 * count), 2 * count), :].astype(F32)
    return block[:count], block[count : count + 1] + block[count + 1 : count + 2] + block[count + 2 : count + 3]


def follow(ref, k, rates, state):
    end, total = unpacked(ref, k, rates.shape[0])
    return jnp.exp2(total * rates) * state + end


def line_kernel(a_ref, b_ref, c_ref, d_ref, rates_ref, ends_ref, sent_ref):
    rates = rates_ref[...]
    count, width = rates.shape
    for k, ref in enumerate((a_ref, b_ref, c_ref, d_ref)):
        ends_ref[2 * count * k : 2 * count * (k + 1), :] = ref[...]
    y = lax.axis_index("ctx") % SIDE_Y

    def one(j, carry):
        state, total = carry
        at = (y + SIDE_Y - j) % SIDE_Y
        end, more = unpacked(ends_ref, at, count)
        return jnp.exp2(more * rates) * state + end, total + more

    state, total = lax.fori_loop(
        0, SIDE_Y, one, (jnp.zeros((count, width), F32), jnp.zeros((1, width), F32))
    )
    sent_ref[...] = packed(state, total)


def scan_kernel(
    rows_ref, ends_ref, maps_ref, codes_ref, drive_ref, signal_ref, rates_ref, skip_ref, gate_ref, proj_ref,
    own_ref, other_ref, out, arranged, gated, proj, sem,
):
    fetch = pltpu.make_async_copy(proj_ref, proj, sem)
    fetch.start()
    rates = rates_ref[...]
    count, width = rates.shape
    ctx, exp = lax.axis_index("ctx"), lax.axis_index("exp")
    x, y = ctx // SIDE_Y, ctx % SIDE_Y

    zero = jnp.zeros((count, width), F32)
    start = lax.fori_loop(0, x, lambda j, state: follow(rows_ref, (x - j), rates, state), zero)
    start = lax.fori_loop(0, y, lambda j, state: follow(ends_ref, (y - j), rates, state), start)
    state = tuple(start[:, i * 128 : (i + 1) * 128] for i in range(width // 128))
    recur(maps_ref, codes_ref, drive_ref, rates, state, out)
    z, c = exp // CORES, exp % CORES

    def gate(j, carry):
        rows = pl.ds(pl.multiple_of(j * GROUP, GROUP), GROUP)
        away = (j // CORES + DEPTH - z) % DEPTH
        to = (j % CORES + c) % CORES * DEPTH + away % 2 * (DEPTH // 2) + away // 2
        value = out[rows, :] + skip_ref[...] * signal_ref[rows, :]
        arranged[pl.ds(pl.multiple_of(to * GROUP, GROUP), GROUP), :] = value * gate_ref[rows, :]
        return carry

    lax.fori_loop(0, codes_ref.shape[0] // GROUP, gate, 0)
    gated[...] = arranged[...].astype(BF16)
    fetch.wait()
    half = own_ref.shape[0]
    step = 512

    def product(k, carry):
        cols = pl.ds(pl.multiple_of(k * step, step), step)
        block = jnp.dot(gated[...], proj[:, cols], preferred_element_type=F32)
        own_ref[:, cols] = block[:half].astype(BF16)
        other_ref[:, cols] = block[half:].astype(BF16)
        return carry

    lax.fori_loop(0, proj.shape[1] // step, product, 0)


def state_space(
    inner_input, gate_input, step_codes, conv_weight, conv_bias, decay_rates, skip_gain, state_proj, out_proj
):
    length, width = inner_input.shape
    taps = conv_weight.shape[0]
    count = decay_rates.shape[0]
    model = out_proj.shape[1]
    border = shifted(inner_input[length - taps + 1 :], "ctx", 1)

    def wide(rows, kind=F32):
        return jax.ShapeDtypeStruct((rows, width), kind)

    maps_shape = jax.ShapeDtypeStruct((2 * count, length), F32)
    conv, codes, gate, taps_in, proj, rates, skip = pl.pallas_call(
        stage_kernel,
        out_shape=(
            wide(length), wide(length), wide(length), wide(taps), wide(2 * count, BF16), wide(count), wide(1),
        ),
        in_specs=[HBM] * 8,
        out_specs=(VMEM,) * 7,
        scratch_shapes=[
            pltpu.VMEM((length, width), BF16),
            pltpu.VMEM((length, width), jnp.int32),
            pltpu.VMEM((length, width), BF16),
            pltpu.VMEM((1, width), F32),
            pltpu.VMEM((count, width), F32),
            pltpu.VMEM((length + 8, width), F32),
            pltpu.SemaphoreType.DMA((8,)),
        ],
        compiler_params=SMALL,
        cost_estimate=pl.CostEstimate(flops=1 << 20, bytes_accessed=8 << 20, transcendentals=1 << 16),
        name="stage",
    )(
        *in_hbm(
            inner_input,
            step_codes,
            gate_input,
            conv_weight,
            conv_bias[None],
            state_proj.T,
            decay_rates,
            skip_gain[None],
        )
    )
    signal, drive, part = pl.pallas_call(
        signal_kernel,
        out_shape=(wide(length), wide(length), maps_shape),
        in_specs=[VMEM] * 5,
        out_specs=(VMEM,) * 3,
        compiler_params=SMALL,
        name="signal",
    )(border, conv, codes, taps_in, proj)
    part = sum(near(part), part)
    maps, sent = pl.pallas_call(
        end_kernel,
        out_shape=(maps_shape, wide(2 * count, BF16)),
        in_specs=[VMEM] * 7,
        out_specs=(VMEM,) * 2,
        compiler_params=SMALL,
        name="end_state",
    )(part, *far([part] * (DEPTH // 2)), codes, drive, rates)
    ends, line = pl.pallas_call(
        line_kernel,
        out_shape=(wide(2 * count * SIDE_Y, BF16), wide(2 * count, BF16)),
        in_specs=[VMEM] * 5,
        out_specs=(VMEM,) * 2,
        compiler_params=SMALL,
        name="line",
    )(sent, *[along_plane(sent, 0, k) for k in range(1, SIDE_Y)], rates)
    rows = join([line] + [along_plane(line, k, 0) for k in range(1, SIDE_X)])
    half = jax.ShapeDtypeStruct((length // 2, model), BF16)
    return pl.pallas_call(
        scan_kernel,
        out_shape=(half, half),
        in_specs=[VMEM] * 9 + [HBM],
        out_specs=(VMEM,) * 2,
        scratch_shapes=[
            pltpu.VMEM((length, width), F32),
            pltpu.VMEM((length, width), F32),
            pltpu.VMEM((length, width), BF16),
            pltpu.VMEM((width, model), BF16),
            pltpu.SemaphoreType.DMA,
        ],
        compiler_params=MEDIUM,
        name="scan",
    )(rows, ends, maps, codes, drive, signal, rates, skip, gate, *in_hbm(out_proj))


def join_kernel(*refs):
    out = refs[-1]
    at = 0
    for ref in refs[:-1]:
        out[at : at + ref.shape[0], :] = ref[...]
        at += ref.shape[0]


def join(arrays):
    rows = sum(a.shape[0] for a in arrays)
    return pl.pallas_call(
        join_kernel,
        out_shape=jax.ShapeDtypeStruct((rows,) + arrays[0].shape[1:], arrays[0].dtype),
        in_specs=[VMEM] * len(arrays),
        out_specs=VMEM,
        compiler_params=SMALL,
        name="join",
    )(*arrays)


def in_hbm(*arrays):
    return [pltpu.with_memory_space_constraint(a, pltpu.HBM) for a in arrays]


def added(*arrays):
    return sum(a.astype(F32) for a in arrays).astype(BF16)


def sum_out(own, other):
    pair = added(own, along_depth(other, lambda z, c: (z, 1 - c)))
    even, up, down = pair[: 4 * GROUP], pair[4 * GROUP : 6 * GROUP], pair[6 * GROUP :]
    low = split(along_depth(up, lambda z, c: (z + 1, c)), 2)
    high = split(along_depth(down, lambda z, c: (z - 1, c)), 2)
    even = split(even, 4)
    blocks = [added(even[0], low[0], high[1]), added(even[1], low[1]), even[2], added(even[3], high[0])]
    return sum((a.astype(F32) for a in far(blocks)), blocks[0].astype(F32))


def expert_kernel(count, *refs):
    pieces, (up_ref, down_ref), outs = refs[:count], refs[count : count + 2], refs[count + 2 : 2 * count + 2]
    rows, hidden = refs[2 * count + 2 :]
    step = 256
    places = []
    at = 0
    for ref in pieces:
        places.append(slice(at, at + ref.shape[0]))
        rows[places[-1], :] = ref[...]
        at += ref.shape[0]
    for k in range(up_ref.shape[1] // step):
        cols = slice(k * step, (k + 1) * step)
        block = jnp.dot(rows[...], up_ref[:, cols], preferred_element_type=F32)
        hidden[:, cols] = silu(block).astype(BF16)

    def down(k, carry):
        cols = pl.ds(pl.multiple_of(k * step, step), step)
        block = jnp.dot(hidden[...], down_ref[:, cols], preferred_element_type=F32).astype(BF16)
        for place, out in zip(places, outs):
            out[:, cols] = block[place]
        return carry

    lax.fori_loop(0, down_ref.shape[1] // step, down, 0)


def expert(pieces, up, down):
    size = sum(p.shape[0] for p in pieces)
    model, width = up.shape
    return pl.pallas_call(
        functools.partial(expert_kernel, len(pieces)),
        out_shape=tuple(jax.ShapeDtypeStruct(p.shape, BF16) for p in pieces),
        in_specs=[VMEM] * (len(pieces) + 2),
        out_specs=(VMEM,) * len(pieces),
        scratch_shapes=[pltpu.VMEM((size, model), BF16), pltpu.VMEM((size, width), BF16)],
        compiler_params=MEDIUM,
        cost_estimate=pl.CostEstimate(
            flops=4 * size * model * width, bytes_accessed=4 * size * model, transcendentals=size * width
        ),
        name="expert",
    )(*pieces, up, down)


def fetch_kernel(after_ref, up_ref, down_ref, up_out, down_out, sems):
    up = pltpu.make_async_copy(up_ref, up_out, sems.at[0])
    down = pltpu.make_async_copy(down_ref, down_out, sems.at[1])
    up.start()
    down.start()
    up.wait()
    down.wait()


def fetch(after, up, down):
    return pl.pallas_call(
        fetch_kernel,
        out_shape=(jax.ShapeDtypeStruct(up.shape, BF16), jax.ShapeDtypeStruct(down.shape, BF16)),
        in_specs=[pl.BlockSpec(memory_space=pl.ANY), HBM, HBM],
        out_specs=(VMEM, VMEM),
        scratch_shapes=[pltpu.SemaphoreType.DMA((2,))],
        compiler_params=SMALL,
        cost_estimate=pl.CostEstimate(flops=0, bytes_accessed=32 << 20, transcendentals=0),
        name="fetch",
    )(after, *in_hbm(up, down))


def split(array, parts):
    size = array.shape[0] // parts
    return [array[k * size : (k + 1) * size] for k in range(parts)]


def swap(array):
    return along_depth(array, lambda z, c: (z, 1 - c))


def along_side(array, side, step):
    pairs = []
    for x in range(SIDE_X):
        for y in range(SIDE_Y):
            for exp in range(DEPTH * CORES):
                if (side + exp) % 2 == 0:
                    to = (x + step) % SIDE_X * SIDE_Y + y
                else:
                    to = x * SIDE_Y + (y + step) % SIDE_Y
                pairs.append(((x * SIDE_Y + y) * DEPTH * CORES + exp, to * DEPTH * CORES + exp))
    return lax.ppermute(array, ("ctx", "exp"), pairs)


def run_expert(mine, theirs, up, down):
    steps = (1, 2, 3)
    base = jnp.concatenate([mine, theirs])
    size = mine.shape[0]
    visits = [base] + [along_side(base, 0, k) for k in steps]
    group = join([v[:size] for v in visits] + [v[size:] for v in visits])
    half = group.shape[0] // 2
    before_theirs = along_side(group[half:], 1, -1)
    after, before_mine = along_side(group, 1, 1), along_side(group[:half], 1, -1)
    up, down = fetch(group, up, down)
    own_mine, own_swapped = expert([group[:half], swap(group[half:])], up, down)
    after, before_mine, up, down, own_mine, own_swapped = lax.optimization_barrier(
        (after, before_mine, up, down, own_mine, own_swapped)
    )
    before_swapped = swap(before_theirs)
    far_mine, far_swapped = along_side(after[:half], 1, 1), along_side(before_swapped, 0, -1)
    close = [after[:half], before_mine, swap(after[half:]), before_swapped]
    far_mine, far_swapped = expert([far_mine, far_swapped], up, down)
    passed_mine, passed_swapped = along_side(far_mine, 1, -1), along_side(far_swapped, 0, 1)
    passed_mine, passed_swapped, own_theirs = lax.optimization_barrier(
        (passed_mine, passed_swapped, swap(own_swapped))
    )
    after_mine, before_mine, after_swapped, before_swapped = expert(close, up, down)
    after_theirs = swap(after_swapped)
    before_theirs = swap(added(before_swapped, passed_swapped))
    one = along_side(jnp.concatenate([added(after_mine, passed_mine), after_theirs]), 1, -1)
    three_mine, three_theirs = along_side(before_mine, 1, 1), along_side(before_theirs, 1, 1)
    total_mine = split(added(own_mine, one[:half], three_mine), 4)
    total_theirs = split(added(own_theirs, one[half:], three_theirs), 4)
    blocks = [jnp.concatenate([m, t]) for m, t in zip(total_mine, total_theirs)]
    return added(blocks[0], *[along_side(blocks[k], 0, -k) for k in steps])


def shards(
    inner_input,
    gate_input,
    step_codes,
    conv_weight,
    conv_bias,
    decay_rates,
    skip_gain,
    state_proj,
    out_proj,
    residual,
    norm_gain,
    expert_ids,
    gate_codes,
    up_weight,
    down_weight,
):
    own, other = state_space(
        inner_input,
        gate_input,
        step_codes,
        conv_weight,
        conv_bias,
        decay_rates,
        skip_gain,
        state_proj,
        out_proj,
    )
    row_count = residual.shape[0]
    mamba_out = sum_out(own, other)
    stream = (residual.astype(F32) + mamba_out).astype(BF16)
    stream_wide = stream.astype(F32)
    normed = (
        stream_wide
        * lax.rsqrt(jnp.mean(stream_wide * stream_wide, axis=-1, keepdims=True) + 1e-05)
        * norm_gain
    ).astype(BF16)
    experts = lax.axis_size("exp") * up_weight.shape[0]
    top_count = expert_ids.shape[1]
    capacity = max(2, 4 * row_count // experts)
    onehot = (
        (expert_ids[:, :, None] == jnp.arange(experts)[None, None, :])
        .astype(jnp.int32)
        .reshape(row_count * top_count, experts)
    )
    before = jnp.cumsum(onehot, axis=0) - onehot
    ranking = jnp.sum(before * onehot, axis=1).reshape(row_count, top_count)
    slot_index = expert_ids // CORES * (CORES * capacity) + ranking * CORES
    slot_index = slot_index + (expert_ids % CORES != ranking).astype(jnp.int32)
    slots = slot_index[:, :, None] == jnp.arange(experts * capacity)[None, None, :]
    dispatch_table = jnp.any(slots, axis=1).astype(BF16)
    up_local = up_weight[0]
    down_local = down_weight[0]
    outgoing = lax.dot_general(
        dispatch_table, normed, (((0,), (0,)), ((), ())), preferred_element_type=F32
    ).astype(BF16)
    outgoing = outgoing.reshape(experts, capacity, -1)
    arrived = lax.all_to_all(outgoing, "exp", split_axis=0, concat_axis=0, tiled=True)
    expert_out = run_expert(arrived[:, 0], arrived[:, 1], up_local, down_local)
    expert_out = jnp.stack(split(expert_out, 2), axis=1)
    returned = lax.all_to_all(expert_out, "exp", split_axis=0, concat_axis=0, tiled=True)
    returned = returned.reshape(experts * capacity, -1)
    gate_weights = gate_codes.astype(F32)
    gate_weights = gate_weights / jnp.sum(gate_weights, axis=1, keepdims=True)
    table = jnp.sum(gate_weights[:, :, None] * slots.astype(F32), axis=1)
    mixture_out = jnp.dot(table, returned.astype(F32), precision=lax.Precision.HIGHEST)
    return (stream_wide + mixture_out).astype(BF16)


def solution(mesh):
    return jax.shard_map(
        shards,
        mesh=mesh,
        in_specs=(
            P("ctx", "exp"),
            P("ctx", "exp"),
            P("ctx", "exp"),
            P(None, "exp"),
            P("exp"),
            P(None, "exp"),
            P("exp"),
            P("exp", None),
            P("exp", None),
            P(("ctx", "exp"), None),
            P(),
            P(("ctx", "exp"), None),
            P(("ctx", "exp"), None),
            P("exp", None, "ctx"),
            P("exp", "ctx", None),
        ),
        out_specs=P(("ctx", "exp"), None),
        check_vma=False,
    )
```
